128 devices in a mesh: seq: 32 (over y, x, core), head: 4 (over z).
Axes of the slice: x: 4, y: 4, z: 4, core: 2. Of those that a mesh axis runs over, the one named last changes fastest.
Arguments:
- tokens: bfloat16 [32768, 768], P('seq'), may hold values from -6 to 6
- cluster_of: int32 [32768], P('seq'), may hold values from 0 to 127, as said below
- w_query: bfloat16 [3, 768, 768], P(None, 'head')
- w_key: bfloat16 [3, 768, 768], P(None, 'head')
- w_value: bfloat16 [3, 768, 768], P(None, 'head'), may hold values from -0.21875 to 0.21875
- w_out: bfloat16 [3, 768, 768], replicated, may hold values from -0.21875 to 0.21875
Outputs:
- mixed: bfloat16 [32768, 768], P('seq')
The draws below stay inside these ranges and needn't reach their ends.
Inputs may be any that keep to these rules, and one draw needn't show every extreme that they name: `cluster_of`: owner k holds the 4 clusters k * 4 to (k + 1) * 4 - 1. Of the 1024 tokens of one device, at most 64 lie in one owner's clusters, and in every draw one owner has exactly 64 tokens from every device.
All inputs are finite; a program needn't handle non-finite values.
Results may differ from the reference program's by a relative error of at most 0.012.
Values may be sent and summed in bfloat16 or wider, within the bound.
A program may use at most 128 MiB of HBM per device.

```python
import math
import jax
import jax.numpy as jnp
from jax import lax

D = 768
HD = 64
HALF = 128
TOK_DEV = 1024
CLU_DEV = 4
TOKENS = 32768
NCLUST = 128
N_SEQ = 32


def draw_w_query(key, part):
    key = jax.random.fold_in(key, 31)
    return (jax.random.normal(key, (3, D, D), jnp.float32) / math.sqrt(D)).astype(jnp.bfloat16)


def draw_w_key(key, part):
    key = jax.random.fold_in(key, 37)
    return (jax.random.normal(key, (3, D, D), jnp.float32) / math.sqrt(D)).astype(jnp.bfloat16)


def draw_cluster_of(key, part):
    key = jax.random.fold_in(key, 9)
    keys = jax.random.split(key, 5)
    owners = NCLUST // CLU_DEV
    sources = TOKENS // TOK_DEV
    pair_rows = 2 * TOK_DEV // owners
    loads = jax.random.randint(keys[0], (owners,), 0, 64)
    heavy = jax.random.randint(keys[1], (), 0, owners)
    owner_slot = jnp.repeat(jnp.arange(owners, dtype=jnp.int32), pair_rows)
    noise = jax.random.randint(keys[2], (sources, owners * pair_rows), 0, 65536)
    scores = noise + loads[owner_slot][None, :] * 2048 + jnp.where(owner_slot == heavy, 4194304, 0)[None, :]
    picked = jnp.argsort(-scores, axis=1, stable=True)[:, :TOK_DEV]
    picked = jax.random.permutation(keys[3], picked, axis=1, independent=True)
    within = jax.random.randint(keys[4], (sources, TOK_DEV), 0, CLU_DEV)
    return (owner_slot[picked] * CLU_DEV + within).reshape(TOKENS).astype(jnp.int32)


def block_scale(key, shape, shards, least, high):
    def one(dim, shards_of):
        heights = jax.random.uniform(jax.random.fold_in(jax.random.fold_in(key, 6), dim), (shards_of,), jnp.float32, least / len(shards), high / len(shards))
        return jnp.repeat(jnp.exp(heights), shape[dim] // shards_of).reshape((-1,) + (1,) * (len(shape) - dim - 1))

    gain = one(*shards[0])
    for cut in shards[1:]:
        gain = gain * one(*cut)
    return gain


def centred(own_key, shape, deviation, most, shards=(), kind=jnp.bfloat16):
    entries = deviation * jax.random.normal(own_key, shape, jnp.float32)
    if shards:
        entries = entries * block_scale(own_key, shape, shards, -0.22, 0.18)
    return jnp.clip(entries, -most, most).astype(kind)


def setup_inputs(seed: int = 0) -> dict:
    seeds = jax.random.split(jax.random.key(seed), 7)
    tokens = centred(seeds[0], (TOKENS, D), 1.0, 6.0, ((0, 32),))
    cluster_of = draw_cluster_of(jax.random.fold_in(seeds[6], 71), 0)
    w_query = draw_w_query(jax.random.fold_in(seeds[6], 71), 0)
    w_key = draw_w_key(jax.random.fold_in(seeds[6], 71), 0)
    w_value = centred(seeds[4], (3, D, D), D ** -0.5, 0.21875, ((1, 4),))
    w_out = centred(seeds[5], (3, D, D), D ** -0.5, 0.21875)
    return dict(tokens=tokens, cluster_of=cluster_of, w_query=w_query, w_key=w_key, w_value=w_value, w_out=w_out)


def row_normed(residual):
    widened = residual.astype(jnp.float32)
    factor = lax.rsqrt(lax.optimization_barrier(jnp.mean(widened * widened, axis=1, keepdims=True)) + 1e-05)
    return (widened * factor).astype(jnp.bfloat16)

def project_rows(normed, matrix):
    return lax.dot_general(normed, matrix, (((1,), (1,)), ((), ())), preferred_element_type=jnp.float32).astype(jnp.bfloat16)

def projections(normed, w_query, w_key, w_value, layer_index):
    return tuple((project_rows(normed, matrix[layer_index]) for matrix in (w_query, w_key, w_value)))

def attend_heads(queries, key_rows, value_rows, permitted):
    query_heads = queries.astype(jnp.float32).reshape(queries.shape[0], -1, HD)
    key_heads = key_rows.astype(jnp.float32).reshape(key_rows.shape[0], -1, HD)
    value_heads = value_rows.astype(jnp.float32).reshape(value_rows.shape[0], -1, HD)
    scores = jnp.einsum('qhe,khe->hqk', query_heads, key_heads) / math.sqrt(HD)
    scores = jnp.where(permitted[None], scores, -1e+30)
    highest = lax.optimization_barrier(jnp.max(scores, axis=2, keepdims=True))
    weights = jnp.where(permitted[None], jnp.exp(scores - highest), 0.0)
    shares = (weights / lax.optimization_barrier(jnp.sum(weights, axis=2, keepdims=True))).astype(jnp.bfloat16)
    result = jnp.einsum('hqk,khe->qhe', shares.astype(jnp.float32), value_heads)
    return result.reshape(queries.shape[0], -1).astype(jnp.bfloat16)

def output_update(residual, attended, w_out, layer_index):
    update = jnp.dot(attended, w_out[layer_index], preferred_element_type=jnp.float32)
    return (residual.astype(jnp.float32) + update).astype(jnp.bfloat16)

def window_layer(residual, w_query, w_key, w_value, w_out, layer_index):
    queries, key_rows, value_rows = projections(row_normed(residual), w_query, w_key, w_value, layer_index)
    total_rows = residual.shape[0]
    padded_keys = jnp.pad(key_rows, ((HALF, HALF), (0, 0)))
    padded_values = jnp.pad(value_rows, ((HALF, HALF), (0, 0)))
    block_rows = min(512, TOK_DEV)

    def one_block(number):
        begin_row = number * block_rows
        query_pos = begin_row + jnp.arange(block_rows, dtype=jnp.int32)
        key_pos = begin_row - HALF + jnp.arange(block_rows + 2 * HALF, dtype=jnp.int32)
        offsets = key_pos[None, :] - query_pos[:, None]
        permitted = (key_pos[None, :] >= 0) & (key_pos[None, :] < total_rows) & (offsets >= -HALF) & (offsets < HALF)
        return attend_heads(lax.dynamic_slice_in_dim(queries, begin_row, block_rows, 0), lax.dynamic_slice_in_dim(padded_keys, begin_row, block_rows + 2 * HALF, 0), lax.dynamic_slice_in_dim(padded_values, begin_row, block_rows + 2 * HALF, 0), permitted)
    attended = lax.map(one_block, jnp.arange(total_rows // block_rows, dtype=jnp.int32)).reshape(total_rows, D)
    return output_update(residual, attended, w_out, layer_index)

def cluster_layer(residual, cluster_of, w_query, w_key, w_value, w_out, layer_index):
    queries, key_rows, value_rows = projections(row_normed(residual), w_query, w_key, w_value, layer_index)
    total_rows = residual.shape[0]
    target = (cluster_of // CLU_DEV).astype(jnp.int32)
    capacity = 2 * TOK_DEV
    block_rows = min(512, capacity)

    def one_owner(owner_index):
        chosen = jnp.argsort(jnp.where(target == owner_index, 0, 1).astype(jnp.int32), stable=True)[:capacity].astype(jnp.int32)
        is_live = target[chosen] == owner_index
        chosen_ids = jnp.where(is_live, cluster_of[chosen], -1)
        own_queries = queries[chosen]
        own_keys = key_rows[chosen]
        own_values = value_rows[chosen]
        pieces = []
        for number in range(capacity // block_rows):
            begin_row = number * block_rows
            permitted = chosen_ids[begin_row:begin_row + block_rows, None] == chosen_ids[None, :]
            pieces.append(attend_heads(own_queries[begin_row:begin_row + block_rows], own_keys, own_values, permitted))
        return (jnp.concatenate(pieces, axis=0), jnp.where(is_live, chosen, total_rows).astype(jnp.int32))
    answered, places = lax.map(one_owner, jnp.arange(N_SEQ, dtype=jnp.int32))
    attended = jnp.zeros((total_rows, D), jnp.bfloat16).at[places.reshape(-1)].set(answered.reshape(-1, D), mode='drop')
    return output_update(residual, attended, w_out, layer_index)

def reference(tokens, cluster_of, w_query, w_key, w_value, w_out):
    first_out = window_layer(tokens, w_query, w_key, w_value, w_out, 0)
    second_out = cluster_layer(first_out, cluster_of, w_query, w_key, w_value, w_out, 1)
    return window_layer(second_out, w_query, w_key, w_value, w_out, 2)
```

```python
import functools
import math

import jax
import jax.numpy as jnp
from jax import lax
from jax.experimental import pallas as pl
from jax.experimental.pallas import tpu as pltpu
from jax.sharding import PartitionSpec as P

MESH = pl.DeviceIdType.MESH
D = 768
ROWS = 1024
HALF = 128
NS = 32
NH = 4
SLOTS = 64
PAIR = 256
NPAIR = ROWS // PAIR
FAR = -1e30
Q_SCALE = math.log2(math.e) / 8.0
VMEM_LIMIT = 60 * 1024 * 1024

NT = (((1,), (1,)), ((), ()))
NN = (((1,), (0,)), ((), ()))


def matmul(a, b, dims=NN):
    return lax.dot_general(a, b, dims, preferred_element_type=jnp.float32)


def lanes(shape):
    return lax.broadcasted_iota(jnp.int32, shape, 1)


def row_normed(rows):
    wide = rows.astype(jnp.float32)
    factor = lax.rsqrt(jnp.mean(wide * wide, axis=1, keepdims=True) + 1e-05)
    return (wide * factor).astype(jnp.bfloat16)


def only_head(rows, h):
    lane = lanes(rows.shape)
    keep = ((lane >= 64 * h) & (lane < 64 * h + 64)) | (lane >= 192)
    return jnp.where(keep, rows, jnp.zeros_like(rows))


def half_turn(rows):
    return pltpu.roll(rows, 64, 1)


def packed_third(third):
    m = third.shape[0] // 2
    return jnp.where(lanes((m, 128)) < 64, half_turn(third[:m]), third[m:])


def load_out_weights(layer, w_out, wo, sems):
    copies = []
    for g in range(NH):
        copies.append(
            pltpu.make_async_copy(
                w_out.at[layer, pl.ds(192 * g, 128)], wo.at[pl.ds(128 * g, 128)], sems.at[2 * g]
            )
        )
        copies.append(
            pltpu.make_async_copy(
                w_out.at[layer, pl.ds(192 * g + 128, 64)],
                wo.at[pl.ds(512 + 64 * g, 64)],
                sems.at[2 * g + 1],
            )
        )
    return copies


def to_peer(att, send_sem, recv_sem, s, h, p, t):
    return pltpu.make_async_remote_copy(
        src_ref=att.at[h, p],
        dst_ref=att.at[h, p],
        send_sem=send_sem.at[p, t],
        recv_sem=recv_sem.at[p, t],
        device_id=(s, lax.rem(h + t, NH)),
        device_id_type=MESH,
    )


def store_and_send(att, send_sem, recv_sem, s, h, p, first, third):
    att[h, p, 0:PAIR, :] = first.astype(jnp.bfloat16)
    att[h, p, PAIR : PAIR + PAIR // 2, :] = packed_third(third).astype(jnp.bfloat16)
    for t in range(1, NH):
        to_peer(att, send_sem, recv_sem, s, h, p, t).start()


def finish_pair(att, send_sem, recv_sem, s, h, p, x_ref, wo, out_ref):
    for t in range(1, NH):
        to_peer(att, send_sem, recv_sem, s, h, p, t).wait()
    half = PAIR // 2
    low = lanes((half, 128)) < 64
    parts = [att[g, p, 0:PAIR, :] for g in range(NH)]
    for g in (0, 2):
        even = att[g, p, PAIR : PAIR + half, :].astype(jnp.float32)
        odd = att[g + 1, p, PAIR : PAIR + half, :].astype(jnp.float32)
        top = jnp.where(low, even, half_turn(odd))
        bottom = jnp.where(low, half_turn(even), odd)
        parts.append(jnp.concatenate([top, bottom], axis=0).astype(jnp.bfloat16))
    gathered = jnp.concatenate(parts, axis=1)
    rows = pl.ds(pl.multiple_of(p * PAIR, PAIR), PAIR)
    total = matmul(gathered, wo[...]) + x_ref[rows, :].astype(jnp.float32)
    out_ref[rows, :] = total.astype(jnp.bfloat16)


def window_kernel(
    layer,
    x_ref,
    wq,
    wk,
    wv,
    w_out,
    out_ref,
    wcat,
    wo,
    halo,
    q_buf,
    k_buf,
    v_buf,
    att,
    w_sems,
    wo_sems,
    halo_send,
    halo_recv,
    send_sem,
    recv_sem,
):
    s = lax.axis_index("seq")
    h = lax.axis_index("head")
    right, left = lax.rem(s + 1, NS), lax.rem(s + NS - 1, NS)
    barrier = pltpu.get_barrier_semaphore()
    for near in (left, right):
        pl.semaphore_signal(barrier, 1, device_id=(near, h), device_id_type=MESH)
    for t in range(1, NH):
        pl.semaphore_signal(barrier, 1, device_id=(s, lax.rem(h + t, NH)), device_id_type=MESH)

    loads = [
        pltpu.make_async_copy(wq.at[layer], wcat.at[pl.ds(0, 192)], w_sems.at[0]),
        pltpu.make_async_copy(wk.at[layer], wcat.at[pl.ds(256, 192)], w_sems.at[1]),
        pltpu.make_async_copy(
            wv.at[layer, pl.ds(0, 128)], wcat.at[pl.ds(512, 128)], w_sems.at[2]
        ),
        pltpu.make_async_copy(
            wv.at[layer, pl.ds(128, 64)], wcat.at[pl.ds(704, 64)], w_sems.at[3]
        ),
    ]
    out_loads = load_out_weights(layer, w_out, wo, wo_sems)
    for copy in loads + out_loads:
        copy.start()
    for start in (192, 448, 640):
        wcat[start : start + 64, :] = jnp.zeros((64, D), jnp.bfloat16)

    pl.semaphore_wait(barrier, NH + 1)
    halos = [
        pltpu.make_async_remote_copy(
            src_ref=x_ref.at[pl.ds(ROWS - HALF, HALF)],
            dst_ref=halo.at[0],
            send_sem=halo_send.at[0],
            recv_sem=halo_recv.at[0],
            device_id=(right, h),
            device_id_type=MESH,
        ),
        pltpu.make_async_remote_copy(
            src_ref=x_ref.at[pl.ds(0, HALF)],
            dst_ref=halo.at[1],
            send_sem=halo_send.at[1],
            recv_sem=halo_recv.at[1],
            device_id=(left, h),
            device_id_type=MESH,
        ),
    ]
    for copy in halos:
        copy.start()
    for copy in loads:
        copy.wait()

    def keep_keys(projected, rows):
        n = projected.shape[0]
        k_buf[rows, :] = projected[:, 0:256].astype(jnp.bfloat16)
        lane = lanes((n, 256))
        ones = (lane >= 128) & (lane < 192)
        v_buf[rows, :] = jnp.where(ones, 1.0, projected[:, 256:512]).astype(jnp.bfloat16)

    def project(p, carry):
        rows = pl.ds(pl.multiple_of(p * PAIR, PAIR), PAIR)
        projected = matmul(row_normed(x_ref[rows, :]), wcat[...], NT)
        q_buf[rows, :] = (projected[:, 0:256] * Q_SCALE).astype(jnp.bfloat16)
        keep_keys(projected[:, 256:768], pl.ds(pl.multiple_of(p * PAIR + HALF, HALF), PAIR))
        return carry

    lax.fori_loop(0, NPAIR, project, 0)

    def attend(p, carry):
        firsts, thirds = [], []
        for b in range(2):
            begin = pl.multiple_of(p * PAIR + b * HALF, HALF)
            queries = q_buf[pl.ds(begin, HALF), :]
            keys = k_buf[pl.ds(begin, 3 * HALF), :]
            values = v_buf[pl.ds(begin, 3 * HALF), :]
            query = lax.broadcasted_iota(jnp.int32, (HALF, 3 * HALF), 0)
            key = lax.broadcasted_iota(jnp.int32, (HALF, 3 * HALF), 1)
            place = s * ROWS + begin - HALF + key
            allowed = (
                (key >= query)
                & (key < query + 2 * HALF)
                & (place >= 0)
                & (place < NS * ROWS)
            )
            bias = jnp.where(allowed, 0.0, FAR)
            stacked = jnp.concatenate([only_head(queries, g) for g in range(3)], axis=0)
            scores = matmul(stacked, keys, NT) + jnp.concatenate([bias] * 3, axis=0)
            highest = jnp.max(scores, axis=1, keepdims=True)
            weights = jnp.exp2(scores - highest).astype(jnp.bfloat16)
            sums = matmul(weights, values)
            scaled = sums * (1.0 / sums[:, 128:129])
            firsts.append(
                jnp.where(
                    lanes((HALF, 128)) < 64, scaled[0:HALF, 0:128], scaled[HALF : 2 * HALF, 0:128]
                )
            )
            thirds.append(scaled[2 * HALF : 3 * HALF, 128:256])
        store_and_send(
            att,
            send_sem,
            recv_sem,
            s,
            h,
            p,
            jnp.concatenate(firsts, axis=0),
            jnp.concatenate(thirds, axis=0),
        )
        return carry

    lax.fori_loop(1, NPAIR - 1, attend, 0)
    for copy in halos:
        copy.wait()

    def edge(side, carry):
        projected = matmul(row_normed(halo[side]), wcat[256:768, :], NT)
        keep_keys(projected, pl.ds(pl.multiple_of(side * (ROWS + HALF), HALF), HALF))
        return attend(side * (NPAIR - 1), carry)

    lax.fori_loop(0, 2, edge, 0)
    for copy in out_loads:
        copy.wait()

    def finish(p, carry):
        finish_pair(att, send_sem, recv_sem, s, h, p, x_ref, wo, out_ref)
        return carry

    lax.fori_loop(1, NPAIR - 1, finish, 0)
    lax.fori_loop(0, 2, lambda side, carry: finish(side * (NPAIR - 1), carry), 0)


def window_layer(layer, x, w_query, w_key, w_value, w_out):
    whole = pl.BlockSpec(memory_space=pltpu.VMEM)
    anywhere = pl.BlockSpec(memory_space=pl.ANY)
    return pl.pallas_call(
        functools.partial(window_kernel, layer),
        out_shape=jax.ShapeDtypeStruct((ROWS, D), jnp.bfloat16),
        in_specs=[whole] + [anywhere] * 4,
        out_specs=whole,
        scratch_shapes=[
            pltpu.VMEM((768, D), jnp.bfloat16),
            pltpu.VMEM((768, D), jnp.bfloat16),
            pltpu.VMEM((2, HALF, D), jnp.bfloat16),
            pltpu.VMEM((ROWS, 256), jnp.bfloat16),
            pltpu.VMEM((ROWS + 2 * HALF, 256), jnp.bfloat16),
            pltpu.VMEM((ROWS + 2 * HALF, 256), jnp.bfloat16),
            pltpu.VMEM((NH, NPAIR, PAIR + PAIR // 2, 128), jnp.bfloat16),
            pltpu.SemaphoreType.DMA((4,)),
            pltpu.SemaphoreType.DMA((2 * NH,)),
            pltpu.SemaphoreType.DMA((2,)),
            pltpu.SemaphoreType.DMA((2,)),
            pltpu.SemaphoreType.DMA((NPAIR, NH)),
            pltpu.SemaphoreType.DMA((NPAIR, NH)),
        ],
        compiler_params=pltpu.CompilerParams(
            collective_id=layer, has_side_effects=True, vmem_limit_bytes=VMEM_LIMIT
        ),
        name=f"window_{layer}",
    )(x, w_query, w_key, w_value, w_out)


GROUP = 4
NGROUP = NS // GROUP
GROWS = GROUP * SLOTS
ANSWER = SLOTS + SLOTS // 2


def cluster_kernel(
    layer,
    x_ref,
    cluster,
    wq,
    wk,
    wv,
    w_out,
    out_ref,
    wcat,
    wo,
    packed,
    slot_col,
    out_kv,
    out_q,
    in_kv,
    in_q,
    k_all,
    v_all,
    answer,
    back,
    back_all,
    att,
    w_sems,
    wo_sems,
    kv_send,
    kv_recv,
    q_send,
    q_recv,
    a_send,
    a_recv,
    send_sem,
    recv_sem,
):
    s = lax.axis_index("seq")
    h = lax.axis_index("head")
    barrier = pltpu.get_barrier_semaphore()

    def greet(i, carry):
        pl.semaphore_signal(barrier, 1, device_id=(lax.rem(s + i, NS), h), device_id_type=MESH)
        return carry

    lax.fori_loop(1, NS, greet, 0)
    for t in range(1, NH):
        pl.semaphore_signal(barrier, 1, device_id=(s, lax.rem(h + t, NH)), device_id_type=MESH)

    loads = [
        pltpu.make_async_copy(wk.at[layer], wcat.at[pl.ds(0, 192)], w_sems.at[0]),
        pltpu.make_async_copy(
            wv.at[layer, pl.ds(0, 128)], wcat.at[pl.ds(256, 128)], w_sems.at[1]
        ),
        pltpu.make_async_copy(
            wq.at[layer, pl.ds(128, 64)], wcat.at[pl.ds(384, 64)], w_sems.at[2]
        ),
        pltpu.make_async_copy(
            wv.at[layer, pl.ds(128, 64)], wcat.at[pl.ds(448, 64)], w_sems.at[3]
        ),
        pltpu.make_async_copy(
            wq.at[layer, pl.ds(0, 128)], wcat.at[pl.ds(512, 128)], w_sems.at[4]
        ),
    ]
    out_loads = load_out_weights(layer, w_out, wo, wo_sems)
    for copy in loads + out_loads:
        copy.start()
    wcat[192:256, :] = jnp.zeros((64, D), jnp.bfloat16)

    ids = cluster[...]
    target = ids // 4
    mine = (target == lax.broadcasted_iota(jnp.int32, (NS, ROWS), 0)).astype(jnp.float32)
    earlier = (
        lax.broadcasted_iota(jnp.int32, (ROWS, ROWS), 0)
        < lax.broadcasted_iota(jnp.int32, (ROWS, ROWS), 1)
    ).astype(jnp.bfloat16)
    before = jnp.sum(matmul(mine.astype(jnp.bfloat16), earlier) * mine, axis=0, keepdims=True)
    slot = target * SLOTS + before.astype(jnp.int32)
    slot_col[...] = jnp.transpose(jnp.broadcast_to(slot.astype(jnp.float32), (128, ROWS)))
    within = jnp.transpose(
        jnp.broadcast_to((ids - 4 * target).astype(jnp.float32), (128, ROWS))
    )

    for copy in loads:
        copy.wait()
    for p in range(NPAIR):
        rows = slice(p * PAIR, p * PAIR + PAIR)
        projected = matmul(row_normed(x_ref[rows, :]), wcat[...], NT)
        lane = lanes((PAIR, 128))
        mark = (within[rows] == (lane - 64).astype(jnp.float32)).astype(jnp.float32)
        packed[rows, 0:128] = projected[:, 0:128].astype(jnp.bfloat16)
        packed[rows, 128:256] = jnp.where(lane < 64, projected[:, 128:256], mark).astype(
            jnp.bfloat16
        )
        packed[rows, 256:384] = projected[:, 256:384].astype(jnp.bfloat16)
        packed[rows, 384:512] = (
            projected[:, 384:512] * jnp.where(lane < 64, Q_SCALE, 1.0)
        ).astype(jnp.bfloat16)
        packed[rows, 512:640] = (projected[:, 512:640] * Q_SCALE).astype(jnp.bfloat16)

    pl.semaphore_wait(barrier, NS + NH - 2)

    def kv_to(k):
        return pltpu.make_async_remote_copy(
            src_ref=out_kv.at[k],
            dst_ref=in_kv.at[s],
            send_sem=kv_send.at[k],
            recv_sem=kv_recv.at[s],
            device_id=(k, h),
            device_id_type=MESH,
        )

    def kv_from(k):
        return pltpu.make_async_remote_copy(
            src_ref=out_kv.at[k],
            dst_ref=in_kv.at[k],
            send_sem=kv_send.at[k],
            recv_sem=kv_recv.at[k],
            device_id=(k, h),
            device_id_type=MESH,
        )

    def q_to(k):
        return pltpu.make_async_remote_copy(
            src_ref=out_q.at[k],
            dst_ref=in_q.at[s],
            send_sem=q_send.at[k],
            recv_sem=q_recv.at[s],
            device_id=(k, h),
            device_id_type=MESH,
        )

    def q_from(k):
        return pltpu.make_async_remote_copy(
            src_ref=out_q.at[k],
            dst_ref=in_q.at[k],
            send_sem=q_send.at[k],
            recv_sem=q_recv.at[k],
            device_id=(k, h),
            device_id_type=MESH,
        )

    def answer_to(k):
        return pltpu.make_async_remote_copy(
            src_ref=answer.at[k],
            dst_ref=back.at[s],
            send_sem=a_send.at[k],
            recv_sem=a_recv.at[s],
            device_id=(k, h),
            device_id_type=MESH,
        )

    def answer_from(k):
        return pltpu.make_async_remote_copy(
            src_ref=answer.at[k],
            dst_ref=back.at[k],
            send_sem=a_send.at[k],
            recv_sem=a_recv.at[k],
            device_id=(k, h),
            device_id_type=MESH,
        )

    my_group = s // GROUP

    def pack(i, carry):
        g = lax.rem(my_group + NGROUP // 2 + i, NGROUP)
        rows = lax.broadcasted_iota(jnp.int32, (GROWS, ROWS), 0) + g * GROWS
        chosen = (rows == slot).astype(jnp.bfloat16)
        filled = matmul(chosen, packed[...]).astype(jnp.bfloat16)
        for j in range(GROUP):
            k = g * GROUP + j
            part = filled[j * SLOTS : (j + 1) * SLOTS]
            out_kv[k] = part[:, 0:512]
            out_q[k] = part[:, 512:640]

            @pl.when(k != s)
            def _():
                kv_to(k).start()

            @pl.when(k == s)
            def _():
                in_kv[k] = part[:, 0:512]
                in_q[k] = part[:, 512:640]

        return carry

    lax.fori_loop(0, NGROUP, pack, 0)

    def send_q(i, carry):
        k = lax.rem(s + NS // 2 + i, NS)

        @pl.when(k != s)
        def _():
            q_to(k).start()

        return carry

    lax.fori_loop(0, NS, send_q, 0)

    def arrive_kv(k, carry):
        @pl.when(k != s)
        def _():
            kv_from(k).wait_recv()

        lane = lanes((SLOTS, 128))
        rows = pl.ds(pl.multiple_of(k * SLOTS, SLOTS), SLOTS)
        tile = in_kv[k, :, 128:256].astype(jnp.float32)
        other = jnp.where(lane < 68, 1.0 - tile, 0.0)
        k_all[rows, 0:128] = in_kv[k, :, 0:128]
        k_all[rows, 128:256] = jnp.where(lane < 64, tile, other).astype(jnp.bfloat16)
        v_all[rows, 0:128] = in_kv[k, :, 256:384]
        v_all[rows, 128:256] = jnp.where(
            lane < 64, jnp.ones_like(in_kv[k, :, 384:512]), in_kv[k, :, 384:512]
        )
        return carry

    lax.fori_loop(0, NS, arrive_kv, 0)

    def attend(i, carry):
        g = lax.rem(my_group + i, NGROUP)
        first = []
        second = []
        for j in range(GROUP):
            k = g * GROUP + j

            @pl.when(k != s)
            def _():
                q_from(k).wait_recv()

            lane = lanes((SLOTS, 128))
            first.append(in_q[k])
            second.append(
                jnp.where(
                    lane < 64,
                    in_kv[k, :, 384:512].astype(jnp.float32),
                    FAR * in_kv[k, :, 128:256].astype(jnp.float32),
                ).astype(jnp.bfloat16)
            )
        queries = jnp.concatenate(
            [jnp.concatenate(first, axis=0), jnp.concatenate(second, axis=0)], axis=1
        )
        scaled = []
        for head in range(3):
            scores = matmul(only_head(queries, head), k_all[...], NT)
            highest = jnp.max(scores, axis=1, keepdims=True)
            weights = jnp.exp2(scores - highest).astype(jnp.bfloat16)
            sums = matmul(weights, v_all[...])
            scaled.append(sums * (1.0 / sums[:, 128:129]))
        firsts = jnp.where(lanes((GROWS, 128)) < 64, scaled[0][:, 0:128], scaled[1][:, 0:128])
        third = scaled[2][:, 128:256]
        for j in range(GROUP):
            k = g * GROUP + j
            rows = slice(j * SLOTS, (j + 1) * SLOTS)
            a_part = firsts[rows].astype(jnp.bfloat16)
            b_part = packed_third(third[rows]).astype(jnp.bfloat16)
            answer[k, 0:SLOTS, :] = a_part
            answer[k, SLOTS:ANSWER, :] = b_part

            @pl.when(k != s)
            def _():
                answer_to(k).start()

            @pl.when(k == s)
            def _():
                back[k, 0:SLOTS, :] = a_part
                back[k, SLOTS:ANSWER, :] = b_part

        return carry

    lax.fori_loop(0, NGROUP, attend, 0)

    def arrive_back(k, carry):
        @pl.when(k != s)
        def _():
            answer_from(k).wait_recv()

        start = pl.multiple_of(k * SLOTS, SLOTS)
        back_all[pl.ds(start, SLOTS), 0:128] = back[k, 0:SLOTS, :]
        third = back[k, SLOTS:ANSWER, :]
        turned = half_turn(third.astype(jnp.float32)).astype(jnp.bfloat16)
        back_all[pl.ds(start, SLOTS), 128:256] = jnp.concatenate([turned, third], axis=0)
        return carry

    lax.fori_loop(0, NS, arrive_back, 0)

    def unpack(p, carry):
        rows = pl.ds(pl.multiple_of(p * PAIR, PAIR), PAIR)
        col = jnp.concatenate([slot_col[rows, :]] * (NS * SLOTS // 128), axis=1)
        chosen = (col == lanes((PAIR, NS * SLOTS)).astype(jnp.float32)).astype(jnp.bfloat16)
        own = matmul(chosen, back_all[...])
        store_and_send(att, send_sem, recv_sem, s, h, p, own[:, 0:128], own[:, 128:256])
        return carry

    lax.fori_loop(0, NPAIR, unpack, 0)
    for copy in out_loads:
        copy.wait()

    def finish(p, carry):
        finish_pair(att, send_sem, recv_sem, s, h, p, x_ref, wo, out_ref)
        return carry

    lax.fori_loop(0, NPAIR, finish, 0)

    def sent(k, carry):
        @pl.when(k != s)
        def _():
            kv_to(k).wait_send()
            q_to(k).wait_send()
            answer_to(k).wait_send()

        return carry

    lax.fori_loop(0, NS, sent, 0)


def cluster_layer(layer, x, cluster_of, w_query, w_key, w_value, w_out):
    whole = pl.BlockSpec(memory_space=pltpu.VMEM)
    anywhere = pl.BlockSpec(memory_space=pl.ANY)
    bf16 = jnp.bfloat16
    return pl.pallas_call(
        functools.partial(cluster_kernel, layer),
        out_shape=jax.ShapeDtypeStruct((ROWS, D), bf16),
        in_specs=[whole] * 2 + [anywhere] * 4,
        out_specs=whole,
        scratch_shapes=[
            pltpu.VMEM((640, D), bf16),
            pltpu.VMEM((768, D), bf16),
            pltpu.VMEM((ROWS, 640), bf16),
            pltpu.VMEM((ROWS, 128), jnp.float32),
            pltpu.VMEM((NS, SLOTS, 512), bf16),
            pltpu.VMEM((NS, SLOTS, 128), bf16),
            pltpu.VMEM((NS, SLOTS, 512), bf16),
            pltpu.VMEM((NS, SLOTS, 128), bf16),
            pltpu.VMEM((NS * SLOTS, 256), bf16),
            pltpu.VMEM((NS * SLOTS, 256), bf16),
            pltpu.VMEM((NS, ANSWER, 128), bf16),
            pltpu.VMEM((NS, ANSWER, 128), bf16),
            pltpu.VMEM((NS * SLOTS, 256), bf16),
            pltpu.VMEM((NH, NPAIR, PAIR + PAIR // 2, 128), bf16),
            pltpu.SemaphoreType.DMA((5,)),
            pltpu.SemaphoreType.DMA((2 * NH,)),
        ]
        + [pltpu.SemaphoreType.DMA((NS,))] * 6
        + [pltpu.SemaphoreType.DMA((NPAIR, NH))] * 2,
        compiler_params=pltpu.CompilerParams(
            collective_id=layer, has_side_effects=True, vmem_limit_bytes=VMEM_LIMIT
        ),
        name=f"cluster_{layer}",
    )(x, cluster_of, w_query, w_key, w_value, w_out)


def shards(tokens, cluster_of, w_query, w_key, w_value, w_out):
    x = window_layer(0, tokens, w_query, w_key, w_value, w_out)
    x = cluster_layer(1, x, cluster_of.reshape(1, ROWS), w_query, w_key, w_value, w_out)
    return window_layer(2, x, w_query, w_key, w_value, w_out)


def solution(mesh):
    placed = (
        P("seq", None),
        P("seq"),
        P(None, "head", None),
        P(None, "head", None),
        P(None, "head", None),
        P(),
    )
    return jax.shard_map(
        shards, mesh=mesh, in_specs=placed, out_specs=P("seq", None), check_vma=False
    )
```

```python
import math
import types

import jax
import jax.numpy as jnp
from jax import lax
from jax.experimental import pallas as pl
from jax.experimental.pallas import tpu as pltpu
from jax.sharding import PartitionSpec as P

MESH = pl.DeviceIdType.MESH
D = 768
ROWS = 1024
HALF = 128
NS = 32
NH = 4
SLOTS = 64
PAIR = 256
NPAIR = ROWS // PAIR
LAST = NH - 1
FAR = -1e30
Q_SCALE = math.log2(math.e) / 8.0
VMEM_LIMIT = 60 * 1024 * 1024

NT = (((1,), (1,)), ((), ()))
NN = (((1,), (0,)), ((), ()))


def matmul(a, b, dims=NN):
    return lax.dot_general(a, b, dims, preferred_element_type=jnp.float32)


def lanes(shape):
    return lax.broadcasted_iota(jnp.int32, shape, 1)


def row_normed(rows):
    wide = rows.astype(jnp.float32)
    factor = lax.rsqrt(jnp.mean(wide * wide, axis=1, keepdims=True) + 1e-05)
    return (wide * factor).astype(jnp.bfloat16)


def only_head(rows, h):
    lane = lanes(rows.shape)
    keep = ((lane >= 64 * h) & (lane < 64 * h + 64)) | (lane >= 192)
    return jnp.where(keep, rows, jnp.zeros_like(rows))


def half_turn(rows):
    return pltpu.roll(rows, 64, 1)


def packed_third(third):
    m = third.shape[0] // 2
    return jnp.where(lanes((m, 128)) < 64, half_turn(third[:m]), third[m:])


GROUP = 4
NGROUP = NS // GROUP
GROWS = GROUP * SLOTS
ANSWER = SLOTS + SLOTS // 2
PACKED = PAIR + PAIR // 2

BF16, F32 = jnp.bfloat16, jnp.float32
DMA = pltpu.SemaphoreType.DMA
SCRATCH = {
    "x0": pltpu.VMEM((ROWS, D), BF16),
    "x1": pltpu.VMEM((ROWS, D), BF16),
    "x2": pltpu.VMEM((PAIR, D), BF16),
    "x3": pltpu.VMEM((ROWS, D), BF16),
    "w0": pltpu.VMEM((768, D), BF16),
    "w1": pltpu.VMEM((640, D), BF16),
    "w2": pltpu.VMEM((NH, 768, D), BF16),
    "wo": pltpu.VMEM((3, 768, D), BF16),
    "halo0": pltpu.VMEM((2, HALF, D), BF16),
    "halo2": pltpu.VMEM((2, HALF, D), BF16),
    "q0": pltpu.VMEM((ROWS, 256), BF16),
    "k0": pltpu.VMEM((ROWS + 2 * HALF, 256), BF16),
    "v0": pltpu.VMEM((ROWS + 2 * HALF, 256), BF16),
    "q2": pltpu.VMEM((NH, PAIR, 256), BF16),
    "k2": pltpu.VMEM((NH, PAIR + 2 * HALF, 256), BF16),
    "v2": pltpu.VMEM((NH, PAIR + 2 * HALF, 256), BF16),
    "att0": pltpu.VMEM((NH, NPAIR, PACKED, 128), BF16),
    "att1": pltpu.VMEM((NH, PACKED, 128), BF16),
    "own1": pltpu.VMEM((NPAIR, PACKED, 128), BF16),
    "chosen": pltpu.VMEM((NS * SLOTS, ROWS), BF16),
    "chosen_back": pltpu.VMEM((ROWS, NS * SLOTS), BF16),
    "within": pltpu.VMEM((ROWS, 128), F32),
    "packed": pltpu.VMEM((ROWS, 640), BF16),
    "out_kv": pltpu.VMEM((NS, SLOTS, 512), BF16),
    "out_q": pltpu.VMEM((NS, SLOTS, 128), BF16),
    "in_kv": pltpu.VMEM((NS, SLOTS, 512), BF16),
    "in_q": pltpu.VMEM((NS, SLOTS, 128), BF16),
    "k_all": pltpu.VMEM((NS * SLOTS, 256), BF16),
    "v_all": pltpu.VMEM((NS * SLOTS, 256), BF16),
    "answer": pltpu.VMEM((NS, ANSWER, 128), BF16),
    "back": pltpu.VMEM((NS, ANSWER, 128), BF16),
    "back_all": pltpu.VMEM((NS * SLOTS, 256), BF16),
    "x_sems": DMA((NPAIR,)),
    "w0_sems": DMA((4,)),
    "w1_sems": DMA((5,)),
    "w2_sems": DMA((4,)),
    "w2_send": DMA((NH, 4)),
    "w2_recv": DMA((NH, 4)),
    "wo_sems": DMA((3, 2 * NH)),
    "halo0_send": DMA((2,)),
    "halo0_recv": DMA((2,)),
    "halo2_send": DMA((2,)),
    "halo2_recv": DMA((2,)),
    "att0_send": DMA((NPAIR, NH)),
    "att0_recv": DMA((NPAIR, NH)),
    "att1_send": DMA((NH,)),
    "att1_recv": DMA((NH,)),
    "kv_send": DMA((NS,)),
    "kv_recv": DMA((NS,)),
    "q_send": DMA((NS,)),
    "q_recv": DMA((NS,)),
    "a_send": DMA((NS,)),
    "a_recv": DMA((NS,)),
    "x3_send": DMA((2, NH)),
    "x3_recv": DMA((2, NH)),
    "out_sems": DMA((2, NH)),
}
N_ARGS = 7


def remote(src, dst, send_sem, recv_sem, device):
    return pltpu.make_async_remote_copy(
        src_ref=src,
        dst_ref=dst,
        send_sem=send_sem,
        recv_sem=recv_sem,
        device_id=device,
        device_id_type=MESH,
    )


def window_loads(source, target, sems):
    wq, wk, wv = source
    return [
        pltpu.make_async_copy(wq, target.at[pl.ds(0, 192)], sems.at[0]),
        pltpu.make_async_copy(wk, target.at[pl.ds(256, 192)], sems.at[1]),
        pltpu.make_async_copy(wv.at[pl.ds(0, 128)], target.at[pl.ds(512, 128)], sems.at[2]),
        pltpu.make_async_copy(wv.at[pl.ds(128, 64)], target.at[pl.ds(704, 64)], sems.at[3]),
    ]


def keep_keys(projected, k_rows, v_rows):
    k_rows[...] = projected[:, 0:256].astype(BF16)
    lane = lanes((projected.shape[0], 256))
    ones = (lane >= 128) & (lane < 192)
    v_rows[...] = jnp.where(ones, 1.0, projected[:, 256:512]).astype(BF16)


def window_block(queries, keys, values, place):
    query = lax.broadcasted_iota(jnp.int32, (HALF, 3 * HALF), 0)
    key = lax.broadcasted_iota(jnp.int32, (HALF, 3 * HALF), 1)
    allowed = (
        (key >= query)
        & (key < query + 2 * HALF)
        & (place + key >= 0)
        & (place + key < NS * ROWS)
    )
    bias = jnp.where(allowed, 0.0, FAR)
    stacked = jnp.concatenate([only_head(queries, g) for g in range(3)], axis=0)
    scores = matmul(stacked, keys, NT) + jnp.concatenate([bias] * 3, axis=0)
    highest = jnp.max(scores, axis=1, keepdims=True)
    weights = jnp.exp2(scores - highest).astype(BF16)
    sums = matmul(weights, values)
    scaled = sums * (1.0 / sums[:, 128:129])
    low = lanes((HALF, 128)) < 64
    first = jnp.where(low, scaled[0:HALF, 0:128], scaled[HALF : 2 * HALF, 0:128])
    return first, scaled[2 * HALF : 3 * HALF, 128:256]


def gathered_rows(blocks):
    half = PAIR // 2
    low = lanes((half, 128)) < 64
    parts = [block[0:PAIR] for block in blocks]
    for g in (0, 2):
        even = blocks[g][PAIR:PACKED].astype(F32)
        odd = blocks[g + 1][PAIR:PACKED].astype(F32)
        top = jnp.where(low, even, half_turn(odd))
        bottom = jnp.where(low, half_turn(even), odd)
        parts.append(jnp.concatenate([top, bottom], axis=0).astype(BF16))
    return jnp.concatenate(parts, axis=1)


def kernel(*refs):
    x_hbm, cluster, wq, wk, wv, w_out, out_hbm = refs[:N_ARGS]
    r = types.SimpleNamespace(**dict(zip(SCRATCH, refs[N_ARGS:])))
    s = lax.axis_index("seq")
    h = lax.axis_index("head")
    up, down = lax.rem(h + 1, NH), lax.rem(h + LAST, NH)
    right, left = lax.rem(s + 1, NS), lax.rem(s + NS - 1, NS)
    after = (lax.rem(s + (h + 1) // NH, NS), up)
    before = (lax.rem(s + NS - (LAST - h) // LAST, NS), down)

    barrier = pltpu.get_barrier_semaphore()

    def greet(i, carry):
        pl.semaphore_signal(barrier, 1, device_id=(lax.rem(s + i, NS), h), device_id_type=MESH)
        return carry

    lax.fori_loop(1, NS, greet, 0)
    for t in range(1, NH):
        pl.semaphore_signal(barrier, 1, device_id=(s, lax.rem(h + t, NH)), device_id_type=MESH)
    for near in (before, after):
        pl.semaphore_signal(barrier, 1, device_id=near, device_id_type=MESH)

    x_loads = [
        pltpu.make_async_copy(
            x_hbm.at[pl.ds(p * PAIR, PAIR)], r.x0.at[pl.ds(p * PAIR, PAIR)], r.x_sems.at[p]
        )
        for p in range(NPAIR)
    ]
    w0_loads = window_loads((wq.at[0], wk.at[0], wv.at[0]), r.w0, r.w0_sems)
    w1_loads = [
        pltpu.make_async_copy(src, r.w1.at[pl.ds(start, size)], r.w1_sems.at[i])
        for i, (src, start, size) in enumerate(
            [
                (wk.at[1], 0, 192),
                (wv.at[1, pl.ds(0, 128)], 256, 128),
                (wq.at[1, pl.ds(128, 64)], 384, 64),
                (wv.at[1, pl.ds(128, 64)], 448, 64),
                (wq.at[1, pl.ds(0, 128)], 512, 128),
            ]
        )
    ]
    w2_loads = window_loads((wq.at[2], wk.at[2], wv.at[2]), r.w2.at[h], r.w2_sems)
    wo_loads = [
        pltpu.make_async_copy(
            w_out.at[layer, pl.ds(192 * g + 128 * i, 128 - 64 * i)],
            r.wo.at[layer, pl.ds(128 * g + (512 - 64 * g) * i, 128 - 64 * i)],
            r.wo_sems.at[layer, 2 * g + i],
        )
        for layer in range(3)
        for g in range(NH)
        for i in range(2)
    ]
    for copy in x_loads + w0_loads + w1_loads + wo_loads + w2_loads:
        copy.start()
    r.w1[192:256, :] = jnp.zeros((64, D), BF16)
    for start in (192, 448, 640):
        r.w0[start : start + 64, :] = jnp.zeros((64, D), BF16)

    def clear(g, carry):
        for start in (192, 448, 640):
            r.w2[g, start : start + 64, :] = jnp.zeros((64, D), BF16)
        return carry

    lax.fori_loop(0, NH, clear, 0)
    for copy in x_loads:
        copy.wait()
    pl.semaphore_wait(barrier, NS - 1 + NH - 1 + 2)

    halos = [
        remote(
            r.x0.at[pl.ds(ROWS - HALF, HALF)],
            r.halo0.at[0],
            r.halo0_send.at[0],
            r.halo0_recv.at[0],
            (right, h),
        ),
        remote(
            r.x0.at[pl.ds(0, HALF)], r.halo0.at[1], r.halo0_send.at[1], r.halo0_recv.at[1], (left, h)
        ),
    ]
    for copy in halos:
        copy.start()
    for copy in w0_loads:
        copy.wait()

    def project0(p, carry):
        rows = pl.ds(pl.multiple_of(p * PAIR, PAIR), PAIR)
        projected = matmul(row_normed(r.x0[rows, :]), r.w0[...], NT)
        r.q0[rows, :] = (projected[:, 0:256] * Q_SCALE).astype(BF16)
        inner = pl.ds(pl.multiple_of(p * PAIR + HALF, HALF), PAIR)
        keep_keys(projected[:, 256:768], r.k0.at[inner], r.v0.at[inner])
        return carry

    lax.fori_loop(0, NPAIR, project0, 0)

    def att0_to(p, t):
        block = r.att0.at[h, p]
        peer = (s, lax.rem(h + t, NH))
        return remote(block, block, r.att0_send.at[p, t], r.att0_recv.at[p, t], peer)

    def att0_on(p, t):
        half = PACKED // 2
        block = r.att0.at[lax.rem(h + NH - t, NH), p, pl.ds(half * (t // 2), half)]
        peer = (s, lax.rem(h + t, NH))
        return remote(block, block, r.att0_send.at[p, t - 1], r.att0_recv.at[p, t - 1], peer)

    def attend0(p, carry):
        firsts, thirds = [], []
        for b in range(2):
            begin = pl.multiple_of(p * PAIR + b * HALF, HALF)
            first, third = window_block(
                r.q0[pl.ds(begin, HALF), :],
                r.k0[pl.ds(begin, 3 * HALF), :],
                r.v0[pl.ds(begin, 3 * HALF), :],
                s * ROWS + begin - HALF,
            )
            firsts.append(first)
            thirds.append(third)
        r.att0[h, p, 0:PAIR, :] = jnp.concatenate(firsts, axis=0).astype(BF16)
        r.att0[h, p, PAIR:PACKED, :] = packed_third(jnp.concatenate(thirds, axis=0)).astype(BF16)
        for t in (1, 3):
            att0_to(p, t).start()
        return carry

    lax.fori_loop(1, NPAIR - 1, attend0, 0)
    for copy in halos:
        copy.wait()

    def edge0(side, carry):
        projected = matmul(row_normed(r.halo0[side]), r.w0[256:768, :], NT)
        outer = pl.ds(pl.multiple_of(side * (ROWS + HALF), HALF), HALF)
        keep_keys(projected, r.k0.at[outer], r.v0.at[outer])
        return attend0(side * (NPAIR - 1), carry)

    lax.fori_loop(0, 2, edge0, 0)

    def in_order(i):
        return lax.rem(i + 1, 3) + 2 * (i // 3)

    def hand_on(i):
        p = in_order(i)
        for t in (1, 3):
            att0_to(p, t).wait_recv()
        for t in (1, 3):
            att0_on(p, t).start()

    hand_on(0)

    ids = cluster[...]
    target = ids // 4
    mine = (target == lax.broadcasted_iota(jnp.int32, (NS, ROWS), 0)).astype(F32)
    earlier = (
        lax.broadcasted_iota(jnp.int32, (ROWS, ROWS), 0)
        < lax.broadcasted_iota(jnp.int32, (ROWS, ROWS), 1)
    ).astype(BF16)
    rank = jnp.sum(matmul(mine.astype(BF16), earlier) * mine, axis=0, keepdims=True)
    slot = target * SLOTS + rank.astype(jnp.int32)
    slot_col = jnp.transpose(jnp.broadcast_to(slot.astype(F32), (128, ROWS)))
    r.within[...] = jnp.transpose(
        jnp.broadcast_to((ids - 4 * target).astype(F32), (128, ROWS))
    )
    for p in range(NPAIR):
        col = jnp.concatenate([slot_col[p * PAIR : (p + 1) * PAIR]] * (NS * SLOTS // 128), axis=1)
        r.chosen_back[p * PAIR : (p + 1) * PAIR, :] = (
            col == lanes((PAIR, NS * SLOTS)).astype(F32)
        ).astype(BF16)

    hand_on(1)

    def choose(g, carry):
        rows = lax.broadcasted_iota(jnp.int32, (GROWS, ROWS), 0) + g * GROWS
        r.chosen[pl.ds(pl.multiple_of(g * GROWS, GROWS), GROWS), :] = (rows == slot).astype(BF16)
        return carry

    lax.fori_loop(0, NGROUP, choose, 0)
    hand_on(2)
    for copy in w1_loads + wo_loads:
        copy.wait()

    def finish0(i, carry):
        p = in_order(i)
        for t in (1, 3):
            att0_on(p, t).wait_recv()
        rows = pl.ds(pl.multiple_of(p * PAIR, PAIR), PAIR)
        gathered = gathered_rows([r.att0[g, p] for g in range(NH)])
        total = matmul(gathered, r.wo[0]) + r.x0[rows, :].astype(F32)
        x1 = total.astype(BF16)
        r.x1[rows, :] = x1
        projected = matmul(row_normed(x1), r.w1[...], NT)
        lane = lanes((PAIR, 128))
        mark = (r.within[rows, :] == (lane - 64).astype(F32)).astype(F32)
        scale = jnp.where(lane < 64, Q_SCALE, 1.0)
        r.packed[rows, 0:128] = projected[:, 0:128].astype(BF16)
        r.packed[rows, 128:256] = jnp.where(lane < 64, projected[:, 128:256], mark).astype(BF16)
        r.packed[rows, 256:384] = projected[:, 256:384].astype(BF16)
        r.packed[rows, 384:512] = (projected[:, 384:512] * scale).astype(BF16)
        r.packed[rows, 512:640] = (projected[:, 512:640] * Q_SCALE).astype(BF16)
        return carry

    lax.fori_loop(0, 1, finish0, 0)
    hand_on(3)
    lax.fori_loop(1, NPAIR, finish0, 0)

    def kv_to(k, source):
        return remote(r.out_kv.at[k], r.in_kv.at[source], r.kv_send.at[k], r.kv_recv.at[source], (k, h))

    def q_to(k, source):
        return remote(r.out_q.at[k], r.in_q.at[source], r.q_send.at[k], r.q_recv.at[source], (k, h))

    def answer_to(k, source):
        return remote(r.answer.at[k], r.back.at[source], r.a_send.at[k], r.a_recv.at[source], (k, h))

    my_group = s // GROUP

    def pack(i, carry):
        g = lax.rem(my_group + NGROUP // 2 + i, NGROUP)
        rows = pl.ds(pl.multiple_of(g * GROWS, GROWS), GROWS)
        filled = matmul(r.chosen[rows, :], r.packed[...]).astype(BF16)
        for j in range(GROUP):
            k = g * GROUP + j
            part = filled[j * SLOTS : (j + 1) * SLOTS]
            r.out_kv[k] = part[:, 0:512]
            r.out_q[k] = part[:, 512:640]

            @pl.when(k != s)
            def _():
                kv_to(k, s).start()

            @pl.when(k == s)
            def _():
                r.in_kv[k] = part[:, 0:512]
                r.in_q[k] = part[:, 512:640]

        return carry

    lax.fori_loop(0, NGROUP, pack, 0)

    def send_q(i, carry):
        k = lax.rem(s + NS // 2 + i, NS)

        @pl.when(k != s)
        def _():
            q_to(k, s).start()

        return carry

    lax.fori_loop(0, NS, send_q, 0)

    for copy in w2_loads:
        copy.wait()

    def w2_to(t, i):
        start, size = ((0, 192), (256, 192), (512, 128), (704, 64))[i]
        block = r.w2.at[h, pl.ds(start, size)]
        peer = (s, lax.rem(h + t, NH))
        return remote(block, block, r.w2_send.at[t, i], r.w2_recv.at[t, i], peer)

    w2_copies = [w2_to(t, i) for t in range(1, NH) for i in range(4)]
    for copy in w2_copies:
        copy.start()

    def arrive_kv(k, carry):
        @pl.when(k != s)
        def _():
            kv_to(k, k).wait_recv()

        lane = lanes((SLOTS, 128))
        rows = pl.ds(pl.multiple_of(k * SLOTS, SLOTS), SLOTS)
        tile = r.in_kv[k, :, 128:256].astype(F32)
        other = jnp.where(lane < 68, 1.0 - tile, 0.0)
        r.k_all[rows, 0:128] = r.in_kv[k, :, 0:128]
        r.k_all[rows, 128:256] = jnp.where(lane < 64, tile, other).astype(BF16)
        r.v_all[rows, 0:128] = r.in_kv[k, :, 256:384]
        r.v_all[rows, 128:256] = jnp.where(
            lane < 64, jnp.ones((SLOTS, 128), BF16), r.in_kv[k, :, 384:512]
        )
        return carry

    lax.fori_loop(0, NS, arrive_kv, 0)

    def attend1(i, carry):
        g = lax.rem(my_group + i, NGROUP)
        first = []
        second = []
        for j in range(GROUP):
            k = g * GROUP + j

            @pl.when(k != s)
            def _():
                q_to(k, k).wait_recv()

            first.append(r.in_q[k])
            second.append(
                jnp.where(
                    lanes((SLOTS, 128)) < 64,
                    r.in_kv[k, :, 384:512].astype(F32),
                    FAR * r.in_kv[k, :, 128:256].astype(F32),
                ).astype(BF16)
            )
        queries = jnp.concatenate(
            [jnp.concatenate(first, axis=0), jnp.concatenate(second, axis=0)], axis=1
        )
        scaled = []
        for head in range(3):
            scores = matmul(only_head(queries, head), r.k_all[...], NT)
            highest = jnp.max(scores, axis=1, keepdims=True)
            weights = jnp.exp2(scores - highest).astype(BF16)
            sums = matmul(weights, r.v_all[...])
            scaled.append(sums * (1.0 / sums[:, 128:129]))
        firsts = jnp.where(lanes((GROWS, 128)) < 64, scaled[0][:, 0:128], scaled[1][:, 0:128])
        third = scaled[2][:, 128:256]
        for j in range(GROUP):
            k = g * GROUP + j
            rows = slice(j * SLOTS, (j + 1) * SLOTS)
            a_part = firsts[rows].astype(BF16)
            b_part = packed_third(third[rows]).astype(BF16)
            r.answer[k, 0:SLOTS, :] = a_part
            r.answer[k, SLOTS:ANSWER, :] = b_part

            @pl.when(k != s)
            def _():
                answer_to(k, s).start()

            @pl.when(k == s)
            def _():
                r.back[k, 0:SLOTS, :] = a_part
                r.back[k, SLOTS:ANSWER, :] = b_part

        return carry

    lax.fori_loop(0, NGROUP, attend1, 0)

    def arrive_back(k, carry):
        @pl.when(k != s)
        def _():
            answer_to(k, k).wait_recv()

        start = pl.multiple_of(k * SLOTS, SLOTS)
        r.back_all[pl.ds(start, SLOTS), 0:128] = r.back[k, 0:SLOTS, :]
        third = r.back[k, SLOTS:ANSWER, :]
        turned = half_turn(third.astype(F32)).astype(BF16)
        r.back_all[pl.ds(start, SLOTS), 128:256] = jnp.concatenate([turned, third], axis=0)
        return carry

    lax.fori_loop(0, NS, arrive_back, 0)

    def att1_to(t):
        peer = lax.rem(h + t, NH)
        return remote(r.own1.at[peer], r.att1.at[h], r.att1_send.at[t], r.att1_recv.at[t], (s, peer))

    def att1_from(t):
        source = lax.rem(h + NH - t, NH)
        return remote(
            r.own1.at[source], r.att1.at[source], r.att1_send.at[t], r.att1_recv.at[t], (s, source)
        )

    def unpack(t):
        p = lax.rem(h + t, NH)
        rows = pl.ds(pl.multiple_of(p * PAIR, PAIR), PAIR)
        own = matmul(r.chosen_back[rows, :], r.back_all[...])
        return p, own[:, 0:128].astype(BF16), packed_third(own[:, 128:256]).astype(BF16)

    for t in (2, 1, 3):
        p, first, third = unpack(t)
        r.own1[p, 0:PAIR, :] = first
        r.own1[p, PAIR:PACKED, :] = third
        att1_to(t).start()
    _, first, third = unpack(0)
    r.att1[h, 0:PAIR, :] = first
    r.att1[h, PAIR:PACKED, :] = third
    for t in range(1, NH):
        att1_from(t).wait_recv()
    quarter = pl.ds(pl.multiple_of(h * PAIR, PAIR), PAIR)
    total = matmul(gathered_rows([r.att1[g] for g in range(NH)]), r.wo[1])
    r.x2[...] = (total + r.x1[quarter, :].astype(F32)).astype(BF16)

    halos2 = [
        remote(
            r.x2.at[pl.ds(PAIR - HALF, HALF)],
            r.halo2.at[0],
            r.halo2_send.at[0],
            r.halo2_recv.at[0],
            after,
        ),
        remote(
            r.x2.at[pl.ds(0, HALF)], r.halo2.at[1], r.halo2_send.at[1], r.halo2_recv.at[1], before
        ),
    ]
    for copy in halos2:
        copy.start()
    for copy in w2_copies:
        copy.wait()
    normed = row_normed(r.x2[...])
    inner = pl.ds(HALF, PAIR)
    for g in range(NH):
        projected = matmul(normed, r.w2[g], NT)
        r.q2[g] = (projected[:, 0:256] * Q_SCALE).astype(BF16)
        keep_keys(projected[:, 256:768], r.k2.at[g, inner], r.v2.at[g, inner])
    for copy in halos2:
        copy.wait()
    normed = row_normed(r.halo2[...].reshape(2 * HALF, D))
    for g in range(NH):
        projected = matmul(normed, r.w2[g, 256:768, :], NT)
        for side in range(2):
            outer = pl.ds(side * (PAIR + HALF), HALF)
            keep_keys(
                projected[side * HALF : (side + 1) * HALF], r.k2.at[g, outer], r.v2.at[g, outer]
            )

    def x3_to(b, t):
        block = r.x3.at[pl.ds(pl.multiple_of(h * PAIR + b * HALF, HALF), HALF)]
        peer = (s, lax.rem(h + t, NH))
        return remote(block, block, r.x3_send.at[b, t], r.x3_recv.at[b, t], peer)

    def x3_on(b, t):
        source = lax.rem(h + NH - t, NH)
        half = HALF // 2
        block = r.x3.at[
            pl.ds(pl.multiple_of(source * PAIR + b * HALF + half * (t // 2), half), half)
        ]
        peer = (s, lax.rem(h + t, NH))
        return remote(block, block, r.x3_send.at[b, t - 1], r.x3_recv.at[b, t - 1], peer)

    def write(b, t):
        rows = pl.ds(pl.multiple_of(lax.rem(h + t, NH) * PAIR + b * HALF, HALF), HALF)
        return pltpu.make_async_copy(r.x3.at[rows], out_hbm.at[rows], r.out_sems.at[b, t])

    for b in range(2):
        begin = b * HALF
        firsts, thirds = [], []
        for g in range(NH):
            first, third = window_block(
                r.q2[g, begin : begin + HALF, :],
                r.k2[g, begin : begin + 3 * HALF, :],
                r.v2[g, begin : begin + 3 * HALF, :],
                s * ROWS + h * PAIR + begin - HALF,
            )
            firsts.append(first)
            thirds.append(third)
        low = lanes((HALF, 128)) < 64
        for g in (0, 2):
            firsts.append(jnp.where(low, half_turn(thirds[g]), thirds[g + 1]))
        gathered = jnp.concatenate([first.astype(BF16) for first in firsts], axis=1)
        total = matmul(gathered, r.wo[2]) + r.x2[begin : begin + HALF, :].astype(F32)
        rows = pl.ds(pl.multiple_of(h * PAIR + begin, HALF), HALF)
        r.x3[rows, :] = total.astype(BF16)
        for t in (1, 3):
            x3_to(b, t).start()
        write(b, 0).start()
    for b in range(2):
        for t in (1, 3):
            x3_to(b, t).wait_recv()
        for t in (1, 3):
            x3_on(b, t).start()
        for t in (1, 3):
            write(b, t).start()
    for b in range(2):
        for t in (1, 3):
            x3_on(b, t).wait_recv()
        write(b, 2).start()

    def sent(k, carry):
        @pl.when(k != s)
        def _():
            kv_to(k, s).wait_send()
            q_to(k, s).wait_send()
            answer_to(k, s).wait_send()

        return carry

    lax.fori_loop(0, NS, sent, 0)
    for p in range(NPAIR):
        for t in (1, 3):
            att0_to(p, t).wait_send()
            att0_on(p, t).wait_send()
    for t in range(1, NH):
        att1_to(t).wait_send()
    for b in range(2):
        for t in (1, 3):
            x3_to(b, t).wait_send()
            x3_on(b, t).wait_send()
        for t in range(NH):
            write(b, t).wait()


def shards(tokens, cluster_of, w_query, w_key, w_value, w_out):
    anywhere = pl.BlockSpec(memory_space=pl.ANY)
    return pl.pallas_call(
        kernel,
        out_shape=jax.ShapeDtypeStruct((ROWS, D), BF16),
        in_specs=[anywhere, pl.BlockSpec(memory_space=pltpu.VMEM)] + [anywhere] * 4,
        out_specs=anywhere,
        scratch_shapes=list(SCRATCH.values()),
        compiler_params=pltpu.CompilerParams(
            collective_id=0, has_side_effects=True, vmem_limit_bytes=VMEM_LIMIT
        ),
        name="three_layers",
    )(tokens, cluster_of.reshape(1, ROWS), w_query, w_key, w_value, w_out)


def solution(mesh):
    placed = (
        P("seq", None),
        P("seq"),
        P(None, "head", None),
        P(None, "head", None),
        P(None, "head", None),
        P(),
    )
    return jax.shard_map(
        shards, mesh=mesh, in_specs=placed, out_specs=P("seq", None), check_vma=False
    )
```

```python
import math
import types

import jax
import jax.numpy as jnp
from jax import lax
from jax.experimental import pallas as pl
from jax.experimental.pallas import tpu as pltpu
from jax.sharding import PartitionSpec as P

MESH = pl.DeviceIdType.MESH
D = 768
ROWS = 1024
HALF = 128
NS = 32
NH = 4
SLOTS = 64
PAIR = 256
NPAIR = ROWS // PAIR
LAST = NH - 1
FAR = -1e30
Q_SCALE = math.log2(math.e) / 8.0
VMEM_LIMIT = 60 * 1024 * 1024

NT = (((1,), (1,)), ((), ()))
NN = (((1,), (0,)), ((), ()))


def matmul(a, b, dims=NN):
    return lax.dot_general(a, b, dims, preferred_element_type=jnp.float32)


def lanes(shape):
    return lax.broadcasted_iota(jnp.int32, shape, 1)


def row_normed(rows):
    wide = rows.astype(jnp.float32)
    factor = lax.rsqrt(jnp.mean(wide * wide, axis=1, keepdims=True) + 1e-05)
    return (wide * factor).astype(jnp.bfloat16)


def only_head(rows, h):
    lane = lanes(rows.shape)
    keep = ((lane >= 64 * h) & (lane < 64 * h + 64)) | (lane >= 192)
    return jnp.where(keep, rows, jnp.zeros_like(rows))


def half_turn(rows):
    return pltpu.roll(rows, 64, 1)


def packed_third(third):
    m = third.shape[0] // 2
    return jnp.where(lanes((m, 128)) < 64, half_turn(third[:m]), third[m:])


NY, NX, NC = 4, 4, 2
GROUP = NX
NGROUP = NS // GROUP
GROWS = GROUP * SLOTS
ANSWER = SLOTS + SLOTS // 2
PACKED = PAIR + PAIR // 2

BF16, F32 = jnp.bfloat16, jnp.float32
DMA = pltpu.SemaphoreType.DMA
SCRATCH = {
    "x0": pltpu.VMEM((ROWS, D), BF16),
    "x1": pltpu.VMEM((ROWS, D), BF16),
    "x2": pltpu.VMEM((PAIR, D), BF16),
    "x3": pltpu.VMEM((ROWS, D), BF16),
    "w0": pltpu.VMEM((768, D), BF16),
    "w1": pltpu.VMEM((640, D), BF16),
    "w2": pltpu.VMEM((NH, 768, D), BF16),
    "wo": pltpu.VMEM((3, 768, D), BF16),
    "halo0": pltpu.VMEM((2, HALF, D), BF16),
    "halo2": pltpu.VMEM((2, HALF, D), BF16),
    "q0": pltpu.VMEM((ROWS, 256), BF16),
    "k0": pltpu.VMEM((ROWS + 2 * HALF, 256), BF16),
    "v0": pltpu.VMEM((ROWS + 2 * HALF, 256), BF16),
    "q2": pltpu.VMEM((NH, PAIR, 256), BF16),
    "k2": pltpu.VMEM((NH, PAIR + 2 * HALF, 256), BF16),
    "v2": pltpu.VMEM((NH, PAIR + 2 * HALF, 256), BF16),
    "att0": pltpu.VMEM((NH, NPAIR, PACKED, 128), BF16),
    "att1": pltpu.VMEM((NH, PACKED, 128), BF16),
    "own1": pltpu.VMEM((NPAIR, PACKED, 128), BF16),
    "chosen": pltpu.VMEM((NS * SLOTS, ROWS), BF16),
    "chosen_back": pltpu.VMEM((ROWS, NS * SLOTS), BF16),
    "within": pltpu.VMEM((ROWS, 128), F32),
    "packed": pltpu.VMEM((ROWS, 640), BF16),
    "out_k": pltpu.VMEM((NX, NY, NC, SLOTS, 256), BF16),
    "out_v": pltpu.VMEM((NY, NX, NC, SLOTS, 256), BF16),
    "out_q": pltpu.VMEM((NX, NY, NC, SLOTS, 128), BF16),
    "mid_k": pltpu.VMEM((NY, NC, NX, SLOTS, 256), BF16),
    "mid_v": pltpu.VMEM((NX, NC, NY, SLOTS, 256), BF16),
    "mid_q": pltpu.VMEM((NY, NC, NX, SLOTS, 128), BF16),
    "in_k": pltpu.VMEM((NY, NC, NX, SLOTS, 256), BF16),
    "in_v": pltpu.VMEM((NY, NC, NX, SLOTS, 256), BF16),
    "in_q": pltpu.VMEM((NY, NC, NX, SLOTS, 128), BF16),
    "q_third": pltpu.VMEM((NY, NC, NX, SLOTS, 128), BF16),
    "scores": pltpu.VMEM((3, GROWS, NS * SLOTS), F32),
    "answer": pltpu.VMEM((NS, ANSWER, 128), BF16),
    "back": pltpu.VMEM((NS, ANSWER, 128), BF16),
    "back_all": pltpu.VMEM((NS * SLOTS, 256), BF16),
    "x_sems": DMA((NPAIR,)),
    "w0_sems": DMA((4,)),
    "w1_sems": DMA((5,)),
    "w2_sems": DMA((4,)),
    "w2_send": DMA((NH, 4)),
    "w2_recv": DMA((NH, 4)),
    "wo_sems": DMA((3, 2 * NH)),
    "halo0_send": DMA((2,)),
    "halo0_recv": DMA((2,)),
    "halo2_send": DMA((2,)),
    "halo2_recv": DMA((2,)),
    "att0_send": DMA((NPAIR, NH)),
    "att0_recv": DMA((NPAIR, NH)),
    "att1_send": DMA((NH,)),
    "att1_recv": DMA((NH,)),
    "k1_send": DMA((NX,)),
    "k1_recv": DMA((NX,)),
    "v1_send": DMA((NY,)),
    "v1_recv": DMA((NY,)),
    "q1_send": DMA((NX,)),
    "q1_recv": DMA((NX,)),
    "k2_send": DMA((NY, NC)),
    "k2_recv": DMA((NY, NC)),
    "v2_send": DMA((NX, NC)),
    "v2_recv": DMA((NX, NC)),
    "q2_send": DMA((NY, NC)),
    "q2_recv": DMA((NY, NC)),
    "a_send": DMA((NS,)),
    "a_recv": DMA((NS,)),
    "x3_send": DMA((2, NH)),
    "x3_recv": DMA((2, NH)),
    "out_sems": DMA((2, NH)),
}
N_ARGS = 7


def remote(src, dst, send_sem, recv_sem, device):
    return pltpu.make_async_remote_copy(
        src_ref=src,
        dst_ref=dst,
        send_sem=send_sem,
        recv_sem=recv_sem,
        device_id=device,
        device_id_type=MESH,
    )


def window_loads(source, target, sems):
    wq, wk, wv = source
    return [
        pltpu.make_async_copy(wq, target.at[pl.ds(0, 192)], sems.at[0]),
        pltpu.make_async_copy(wk, target.at[pl.ds(256, 192)], sems.at[1]),
        pltpu.make_async_copy(wv.at[pl.ds(0, 128)], target.at[pl.ds(512, 128)], sems.at[2]),
        pltpu.make_async_copy(wv.at[pl.ds(128, 64)], target.at[pl.ds(704, 64)], sems.at[3]),
    ]


def keep_keys(projected, k_rows, v_rows):
    k_rows[...] = projected[:, 0:256].astype(BF16)
    lane = lanes((projected.shape[0], 256))
    ones = (lane >= 128) & (lane < 192)
    v_rows[...] = jnp.where(ones, 1.0, projected[:, 256:512]).astype(BF16)


def window_block(queries, keys, values, place):
    query = lax.broadcasted_iota(jnp.int32, (HALF, 3 * HALF), 0)
    key = lax.broadcasted_iota(jnp.int32, (HALF, 3 * HALF), 1)
    allowed = (
        (key >= query)
        & (key < query + 2 * HALF)
        & (place + key >= 0)
        & (place + key < NS * ROWS)
    )
    bias = jnp.where(allowed, 0.0, FAR)
    stacked = jnp.concatenate([only_head(queries, g) for g in range(3)], axis=0)
    scores = matmul(stacked, keys, NT) + jnp.concatenate([bias] * 3, axis=0)
    highest = jnp.max(scores, axis=1, keepdims=True)
    weights = jnp.exp2(scores - highest).astype(BF16)
    sums = matmul(weights, values)
    scaled = sums * (1.0 / sums[:, 128:129])
    low = lanes((HALF, 128)) < 64
    first = jnp.where(low, scaled[0:HALF, 0:128], scaled[HALF : 2 * HALF, 0:128])
    return first, scaled[2 * HALF : 3 * HALF, 128:256]


def gathered_rows(blocks):
    half = PAIR // 2
    low = lanes((half, 128)) < 64
    parts = [block[0:PAIR] for block in blocks]
    for g in (0, 2):
        even = blocks[g][PAIR:PACKED].astype(F32)
        odd = blocks[g + 1][PAIR:PACKED].astype(F32)
        top = jnp.where(low, even, half_turn(odd))
        bottom = jnp.where(low, half_turn(even), odd)
        parts.append(jnp.concatenate([top, bottom], axis=0).astype(BF16))
    return jnp.concatenate(parts, axis=1)


def kernel(*refs):
    x_hbm, cluster, wq, wk, wv, w_out, out_hbm = refs[:N_ARGS]
    r = types.SimpleNamespace(**dict(zip(SCRATCH, refs[N_ARGS:])))
    s = lax.axis_index("seq")
    h = lax.axis_index("head")
    up, down = lax.rem(h + 1, NH), lax.rem(h + LAST, NH)
    right, left = lax.rem(s + 1, NS), lax.rem(s + NS - 1, NS)
    after = (lax.rem(s + (h + 1) // NH, NS), up)
    before = (lax.rem(s + NS - (LAST - h) // LAST, NS), down)

    barrier = pltpu.get_barrier_semaphore()

    def greet(i, carry):
        pl.semaphore_signal(barrier, 1, device_id=(lax.rem(s + i, NS), h), device_id_type=MESH)
        return carry

    lax.fori_loop(1, NS, greet, 0)
    for t in range(1, NH):
        pl.semaphore_signal(barrier, 1, device_id=(s, lax.rem(h + t, NH)), device_id_type=MESH)
    for near in (before, after):
        pl.semaphore_signal(barrier, 1, device_id=near, device_id_type=MESH)

    x_loads = [
        pltpu.make_async_copy(
            x_hbm.at[pl.ds(p * PAIR, PAIR)], r.x0.at[pl.ds(p * PAIR, PAIR)], r.x_sems.at[p]
        )
        for p in range(NPAIR)
    ]
    w0_loads = window_loads((wq.at[0], wk.at[0], wv.at[0]), r.w0, r.w0_sems)
    w1_loads = [
        pltpu.make_async_copy(src, r.w1.at[pl.ds(start, size)], r.w1_sems.at[i])
        for i, (src, start, size) in enumerate(
            [
                (wk.at[1], 0, 192),
                (wv.at[1, pl.ds(0, 128)], 256, 128),
                (wq.at[1, pl.ds(128, 64)], 384, 64),
                (wv.at[1, pl.ds(128, 64)], 448, 64),
                (wq.at[1, pl.ds(0, 128)], 512, 128),
            ]
        )
    ]
    w2_loads = window_loads((wq.at[2], wk.at[2], wv.at[2]), r.w2.at[h], r.w2_sems)
    wo_loads = [
        pltpu.make_async_copy(
            w_out.at[layer, pl.ds(192 * g + 128 * i, 128 - 64 * i)],
            r.wo.at[layer, pl.ds(128 * g + (512 - 64 * g) * i, 128 - 64 * i)],
            r.wo_sems.at[layer, 2 * g + i],
        )
        for layer in range(3)
        for g in range(NH)
        for i in range(2)
    ]
    for copy in x_loads + w0_loads + w1_loads + wo_loads + w2_loads:
        copy.start()
    r.w1[192:256, :] = jnp.zeros((64, D), BF16)
    for start in (192, 448, 640):
        r.w0[start : start + 64, :] = jnp.zeros((64, D), BF16)

    def clear(g, carry):
        for start in (192, 448, 640):
            r.w2[g, start : start + 64, :] = jnp.zeros((64, D), BF16)
        return carry

    lax.fori_loop(0, NH, clear, 0)
    for copy in x_loads:
        copy.wait()
    pl.semaphore_wait(barrier, NS - 1 + NH - 1 + 2)

    halos = [
        remote(
            r.x0.at[pl.ds(ROWS - HALF, HALF)],
            r.halo0.at[0],
            r.halo0_send.at[0],
            r.halo0_recv.at[0],
            (right, h),
        ),
        remote(
            r.x0.at[pl.ds(0, HALF)], r.halo0.at[1], r.halo0_send.at[1], r.halo0_recv.at[1], (left, h)
        ),
    ]
    for copy in halos:
        copy.start()
    for copy in w0_loads:
        copy.wait()

    def project0(p, carry):
        rows = pl.ds(pl.multiple_of(p * PAIR, PAIR), PAIR)
        projected = matmul(row_normed(r.x0[rows, :]), r.w0[...], NT)
        r.q0[rows, :] = (projected[:, 0:256] * Q_SCALE).astype(BF16)
        inner = pl.ds(pl.multiple_of(p * PAIR + HALF, HALF), PAIR)
        keep_keys(projected[:, 256:768], r.k0.at[inner], r.v0.at[inner])
        return carry

    lax.fori_loop(0, NPAIR, project0, 0)

    def att0_to(p, t):
        block = r.att0.at[h, p]
        peer = (s, lax.rem(h + t, NH))
        return remote(block, block, r.att0_send.at[p, t], r.att0_recv.at[p, t], peer)

    def att0_on(p, t):
        half = PACKED // 2
        block = r.att0.at[lax.rem(h + NH - t, NH), p, pl.ds(half * (t // 2), half)]
        peer = (s, lax.rem(h + t, NH))
        return remote(block, block, r.att0_send.at[p, t - 1], r.att0_recv.at[p, t - 1], peer)

    def attend0(p, carry):
        firsts, thirds = [], []
        for b in range(2):
            begin = pl.multiple_of(p * PAIR + b * HALF, HALF)
            first, third = window_block(
                r.q0[pl.ds(begin, HALF), :],
                r.k0[pl.ds(begin, 3 * HALF), :],
                r.v0[pl.ds(begin, 3 * HALF), :],
                s * ROWS + begin - HALF,
            )
            firsts.append(first)
            thirds.append(third)
        r.att0[h, p, 0:PAIR, :] = jnp.concatenate(firsts, axis=0).astype(BF16)
        r.att0[h, p, PAIR:PACKED, :] = packed_third(jnp.concatenate(thirds, axis=0)).astype(BF16)
        for t in (1, 3):
            att0_to(p, t).start()
        return carry

    lax.fori_loop(1, NPAIR - 1, attend0, 0)
    for copy in halos:
        copy.wait()

    def edge0(side, carry):
        projected = matmul(row_normed(r.halo0[side]), r.w0[256:768, :], NT)
        outer = pl.ds(pl.multiple_of(side * (ROWS + HALF), HALF), HALF)
        keep_keys(projected, r.k0.at[outer], r.v0.at[outer])
        return attend0(side * (NPAIR - 1), carry)

    lax.fori_loop(0, 2, edge0, 0)

    def in_order(i):
        return lax.rem(i + 1, 3) + 2 * (i // 3)

    def hand_on(i):
        p = in_order(i)
        for t in (1, 3):
            att0_to(p, t).wait_recv()
        for t in (1, 3):
            att0_on(p, t).start()

    hand_on(0)

    ids = cluster[...]
    target = ids // 4
    mine = (target == lax.broadcasted_iota(jnp.int32, (NS, ROWS), 0)).astype(F32)
    earlier = (
        lax.broadcasted_iota(jnp.int32, (ROWS, ROWS), 0)
        < lax.broadcasted_iota(jnp.int32, (ROWS, ROWS), 1)
    ).astype(BF16)
    rank = jnp.sum(matmul(mine.astype(BF16), earlier) * mine, axis=0, keepdims=True)
    slot = target * SLOTS + rank.astype(jnp.int32)
    slot_col = jnp.transpose(jnp.broadcast_to(slot.astype(F32), (128, ROWS)))
    r.within[...] = jnp.transpose(
        jnp.broadcast_to((ids - 4 * target).astype(F32), (128, ROWS))
    )
    for p in range(NPAIR):
        col = jnp.concatenate([slot_col[p * PAIR : (p + 1) * PAIR]] * (NS * SLOTS // 128), axis=1)
        r.chosen_back[p * PAIR : (p + 1) * PAIR, :] = (
            col == lanes((PAIR, NS * SLOTS)).astype(F32)
        ).astype(BF16)

    hand_on(1)

    def choose(g, carry):
        rows = lax.broadcasted_iota(jnp.int32, (GROWS, ROWS), 0) + g * GROWS
        r.chosen[pl.ds(pl.multiple_of(g * GROWS, GROWS), GROWS), :] = (rows == slot).astype(BF16)
        return carry

    lax.fori_loop(0, NGROUP, choose, 0)
    hand_on(2)
    for copy in w1_loads + wo_loads:
        copy.wait()

    def finish0(i, carry):
        p = in_order(i)
        for t in (1, 3):
            att0_on(p, t).wait_recv()
        rows = pl.ds(pl.multiple_of(p * PAIR, PAIR), PAIR)
        gathered = gathered_rows([r.att0[g, p] for g in range(NH)])
        total = matmul(gathered, r.wo[0]) + r.x0[rows, :].astype(F32)
        x1 = total.astype(BF16)
        r.x1[rows, :] = x1
        projected = matmul(row_normed(x1), r.w1[...], NT)
        lane = lanes((PAIR, 128))
        mark = (r.within[rows, :] == (lane - 64).astype(F32)).astype(F32)
        scale = jnp.where(lane < 64, Q_SCALE, 1.0)
        r.packed[rows, 0:128] = projected[:, 0:128].astype(BF16)
        r.packed[rows, 128:256] = jnp.where(lane < 64, projected[:, 128:256], mark).astype(BF16)
        r.packed[rows, 256:384] = projected[:, 256:384].astype(BF16)
        r.packed[rows, 384:512] = (projected[:, 384:512] * scale).astype(BF16)
        r.packed[rows, 512:640] = (projected[:, 512:640] * Q_SCALE).astype(BF16)
        return carry

    lax.fori_loop(0, 1, finish0, 0)
    hand_on(3)
    lax.fori_loop(1, NPAIR, finish0, 0)

    y, x, c = s // (NX * NC), lax.rem(s // NC, NX), lax.rem(s, NC)

    def device(y_at, x_at, c_at):
        return (lax.rem(y_at, NY) * (NX * NC) + lax.rem(x_at, NX) * NC + lax.rem(c_at, NC), h)

    def along_x(out, mid, send, recv, d):
        column = lax.rem(x + d, NX)
        return remote(out.at[column], mid.at[:, :, x], send.at[d], recv.at[d], device(y, x + d, c))

    def along_y(out, mid, send, recv, d):
        row = lax.rem(y + d, NY)
        return remote(out.at[row], mid.at[:, :, y], send.at[d], recv.at[d], device(y + d, x, c))

    def k1(d):
        return along_x(r.out_k, r.mid_k, r.k1_send, r.k1_recv, d)

    def q1(d):
        return along_x(r.out_q, r.mid_q, r.q1_send, r.q1_recv, d)

    def v1(d):
        return along_y(r.out_v, r.mid_v, r.v1_send, r.v1_recv, d)

    def then_y(mid, into, send, recv, d, e):
        block = mid.at[lax.rem(y + d, NY), lax.rem(c + e, NC)]
        peer = device(y + d, x, c + e)
        return remote(block, into.at[y, c], send.at[d, e], recv.at[d, e], peer)

    def k2(d, e):
        return then_y(r.mid_k, r.in_k, r.k2_send, r.k2_recv, d, e)

    def q2(d, e):
        return then_y(r.mid_q, r.in_q, r.q2_send, r.q2_recv, d, e)

    def v2(d, e):
        block = r.mid_v.at[lax.rem(x + d, NX), lax.rem(c + e, NC)]
        peer = device(y, x + d, c + e)
        return remote(block, r.in_v.at[:, c, x], r.v2_send.at[d, e], r.v2_recv.at[d, e], peer)

    def answer_to(k, source):
        return remote(r.answer.at[k], r.back.at[source], r.a_send.at[k], r.a_recv.at[source], (k, h))

    def column_rows(column):
        return jnp.concatenate(
            [
                r.chosen[
                    pl.ds(pl.multiple_of((NX * n + column) * NC * SLOTS, NC * SLOTS), NC * SLOTS), :
                ]
                for n in range(NY)
            ],
            axis=0,
        )

    def pack(i, carry):
        d = lax.rem(i + 2, NX)
        column, row = lax.rem(x + d, NX), lax.rem(y + d, NY)
        keys = matmul(column_rows(column), r.packed[:, 0:256])
        lane = lanes(keys.shape)
        keys = jnp.where(lane < 192, keys, jnp.where(lane < 192 + 4, 1.0 - keys, 0.0))
        keys = keys.astype(BF16).reshape(NY, NC, SLOTS, 256)
        size = NX * NC * SLOTS
        rows = pl.ds(pl.multiple_of(row * size, size), size)
        values = matmul(r.chosen[rows, :], r.packed[:, 256:512])
        values = values.astype(BF16).reshape(NX, NC, SLOTS, 256)

        @pl.when(d != 0)
        def _():
            r.out_k[column] = keys
            k1(d).start()
            r.out_v[row] = values
            v1(d).start()

        @pl.when(d == 0)
        def _():
            for n in range(NY):
                for e in range(NC):
                    r.mid_k[n, e, x] = keys[n, e]
                    r.mid_v[n, e, y] = values[n, e]

        return carry

    lax.fori_loop(0, NX, pack, 0)

    def pack_q(i, carry):
        d = lax.rem(i + 2, NX)
        column = lax.rem(x + d, NX)
        queries = matmul(column_rows(column), r.packed[:, 512:640])
        queries = queries.astype(BF16).reshape(NY, NC, SLOTS, 128)

        @pl.when(d != 0)
        def _():
            r.out_q[column] = queries
            q1(d).start()

        @pl.when(d == 0)
        def _():
            for n in range(NY):
                for e in range(NC):
                    r.mid_q[n, e, x] = queries[n, e]

        return carry

    lax.fori_loop(0, NX, pack_q, 0)
    others = [(d, e) for d in (2, 1, 3, 0) for e in range(NC) if (d, e) != (0, 0)]
    for first, then in ((k1, k2), (v1, v2), (q1, q2)):
        for d in (1, 2, 3):
            first(d).wait_recv()
        for d, e in others:
            then(d, e).start()

    for copy in w2_loads:
        copy.wait()

    def w2_to(t, i):
        start, size = ((0, 192), (256, 192), (512, 128), (704, 64))[i]
        block = r.w2.at[h, pl.ds(start, size)]
        peer = (s, lax.rem(h + t, NH))
        return remote(block, block, r.w2_send.at[t, i], r.w2_recv.at[t, i], peer)

    w2_copies = [w2_to(t, i) for t in range(1, NH) for i in range(4)]
    for copy in w2_copies:
        copy.start()

    r.in_k[y, c] = r.mid_k[y, c]
    r.in_q[y, c] = r.mid_q[y, c]
    for n in range(NY):
        r.in_v[n, c, x] = r.mid_v[x, c, n]
    for then in (k2, v2, q2):
        for d, e in others:
            then(d, e).wait_recv()

    def settle(g, carry):
        at = (g // NC, lax.rem(g, NC))
        lane = lax.broadcasted_iota(jnp.int32, (NX, SLOTS, 128), 2)
        other = r.in_k[(*at, slice(None), slice(None), slice(128, 256))].astype(F32)
        third = r.in_v[(*at, slice(None), slice(None), slice(128, 256))]
        marks = jnp.where(lane < 68, FAR * (1.0 - other), 0.0)
        r.q_third[at] = jnp.where(lane < 64, third.astype(F32), marks).astype(BF16)
        r.in_v[(*at, slice(None), slice(None), slice(128, 256))] = jnp.where(
            lane < 64, jnp.ones_like(third), third
        )
        return carry

    lax.fori_loop(0, NGROUP, settle, 0)
    my_group = y * NC + c

    def score(i, head):
        g = lax.rem(my_group + i, NGROUP)
        at = (g // NC, lax.rem(g, NC))
        queries = jnp.concatenate(
            [r.in_q[at].reshape(GROWS, 128), r.q_third[at].reshape(GROWS, 128)], axis=1
        )
        keys = r.in_k[...].reshape(NS * SLOTS, 256)
        r.scores[head] = matmul(only_head(queries, head), keys, NT)

    def weigh(head):
        scores = r.scores[head]
        highest = jnp.max(scores, axis=1, keepdims=True)
        weights = jnp.exp2(scores - highest).astype(BF16)
        sums = matmul(weights, r.in_v[...].reshape(NS * SLOTS, 256))
        return sums * (1.0 / sums[:, 128:129])

    score(0, 0)

    def attend1(i, carry):
        g = lax.rem(my_group + i, NGROUP)
        scaled = []
        for head in range(3):
            score(i + (head + 1) // 3, (head + 1) % 3)
            scaled.append(weigh(head))
        firsts = jnp.where(lanes((GROWS, 128)) < 64, scaled[0][:, 0:128], scaled[1][:, 0:128])
        third = scaled[2][:, 128:256]
        for j in range(GROUP):
            k = (g // NC) * (NX * NC) + j * NC + lax.rem(g, NC)
            rows = slice(j * SLOTS, (j + 1) * SLOTS)
            a_part = firsts[rows].astype(BF16)
            b_part = packed_third(third[rows]).astype(BF16)
            r.answer[k, 0:SLOTS, :] = a_part
            r.answer[k, SLOTS:ANSWER, :] = b_part

            @pl.when(k != s)
            def _():
                answer_to(k, s).start()

            @pl.when(k == s)
            def _():
                r.back[k, 0:SLOTS, :] = a_part
                r.back[k, SLOTS:ANSWER, :] = b_part

        return carry

    lax.fori_loop(0, NGROUP, attend1, 0)

    def arrive_back(k, carry):
        @pl.when(k != s)
        def _():
            answer_to(k, k).wait_recv()

        start = pl.multiple_of(k * SLOTS, SLOTS)
        r.back_all[pl.ds(start, SLOTS), 0:128] = r.back[k, 0:SLOTS, :]
        third = r.back[k, SLOTS:ANSWER, :]
        turned = half_turn(third.astype(F32)).astype(BF16)
        r.back_all[pl.ds(start, SLOTS), 128:256] = jnp.concatenate([turned, third], axis=0)
        return carry

    lax.fori_loop(0, NS, arrive_back, 0)

    def att1_to(t):
        peer = lax.rem(h + t, NH)
        return remote(r.own1.at[peer], r.att1.at[h], r.att1_send.at[t], r.att1_recv.at[t], (s, peer))

    def att1_from(t):
        source = lax.rem(h + NH - t, NH)
        return remote(
            r.own1.at[source], r.att1.at[source], r.att1_send.at[t], r.att1_recv.at[t], (s, source)
        )

    def unpack(t):
        p = lax.rem(h + t, NH)
        rows = pl.ds(pl.multiple_of(p * PAIR, PAIR), PAIR)
        own = matmul(r.chosen_back[rows, :], r.back_all[...])
        return p, own[:, 0:128].astype(BF16), packed_third(own[:, 128:256]).astype(BF16)

    for t in (2, 1, 3):
        p, first, third = unpack(t)
        r.own1[p, 0:PAIR, :] = first
        r.own1[p, PAIR:PACKED, :] = third
        att1_to(t).start()
    _, first, third = unpack(0)
    r.att1[h, 0:PAIR, :] = first
    r.att1[h, PAIR:PACKED, :] = third
    for t in range(1, NH):
        att1_from(t).wait_recv()
    quarter = pl.ds(pl.multiple_of(h * PAIR, PAIR), PAIR)
    total = matmul(gathered_rows([r.att1[g] for g in range(NH)]), r.wo[1])
    r.x2[...] = (total + r.x1[quarter, :].astype(F32)).astype(BF16)

    halos2 = [
        remote(
            r.x2.at[pl.ds(PAIR - HALF, HALF)],
            r.halo2.at[0],
            r.halo2_send.at[0],
            r.halo2_recv.at[0],
            after,
        ),
        remote(
            r.x2.at[pl.ds(0, HALF)], r.halo2.at[1], r.halo2_send.at[1], r.halo2_recv.at[1], before
        ),
    ]
    for copy in halos2:
        copy.start()
    for copy in w2_copies:
        copy.wait()
    normed = row_normed(r.x2[...])
    inner = pl.ds(HALF, PAIR)
    for g in range(NH):
        projected = matmul(normed, r.w2[g], NT)
        r.q2[g] = (projected[:, 0:256] * Q_SCALE).astype(BF16)
        keep_keys(projected[:, 256:768], r.k2.at[g, inner], r.v2.at[g, inner])
    for copy in halos2:
        copy.wait()
    normed = row_normed(r.halo2[...].reshape(2 * HALF, D))
    for g in range(NH):
        projected = matmul(normed, r.w2[g, 256:768, :], NT)
        for side in range(2):
            outer = pl.ds(side * (PAIR + HALF), HALF)
            keep_keys(
                projected[side * HALF : (side + 1) * HALF], r.k2.at[g, outer], r.v2.at[g, outer]
            )

    def x3_to(b, t):
        block = r.x3.at[pl.ds(pl.multiple_of(h * PAIR + b * HALF, HALF), HALF)]
        peer = (s, lax.rem(h + t, NH))
        return remote(block, block, r.x3_send.at[b, t], r.x3_recv.at[b, t], peer)

    def x3_on(b, t):
        source = lax.rem(h + NH - t, NH)
        half = HALF // 2
        block = r.x3.at[
            pl.ds(pl.multiple_of(source * PAIR + b * HALF + half * (t // 2), half), half)
        ]
        peer = (s, lax.rem(h + t, NH))
        return remote(block, block, r.x3_send.at[b, t - 1], r.x3_recv.at[b, t - 1], peer)

    def write(b, t):
        rows = pl.ds(pl.multiple_of(lax.rem(h + t, NH) * PAIR + b * HALF, HALF), HALF)
        return pltpu.make_async_copy(r.x3.at[rows], out_hbm.at[rows], r.out_sems.at[b, t])

    for b in range(2):
        begin = b * HALF
        firsts, thirds = [], []
        for g in range(NH):
            first, third = window_block(
                r.q2[g, begin : begin + HALF, :],
                r.k2[g, begin : begin + 3 * HALF, :],
                r.v2[g, begin : begin + 3 * HALF, :],
                s * ROWS + h * PAIR + begin - HALF,
            )
            firsts.append(first)
            thirds.append(third)
        low = lanes((HALF, 128)) < 64
        for g in (0, 2):
            firsts.append(jnp.where(low, half_turn(thirds[g]), thirds[g + 1]))
        gathered = jnp.concatenate([first.astype(BF16) for first in firsts], axis=1)
        total = matmul(gathered, r.wo[2]) + r.x2[begin : begin + HALF, :].astype(F32)
        rows = pl.ds(pl.multiple_of(h * PAIR + begin, HALF), HALF)
        r.x3[rows, :] = total.astype(BF16)
        for t in (1, 3):
            x3_to(b, t).start()
        write(b, 0).start()
    for b in range(2):
        for t in (1, 3):
            x3_to(b, t).wait_recv()
        for t in (1, 3):
            x3_on(b, t).start()
        for t in (1, 3):
            write(b, t).start()
    for b in range(2):
        for t in (1, 3):
            x3_on(b, t).wait_recv()
        write(b, 2).start()

    def sent(k, carry):
        @pl.when(k != s)
        def _():
            answer_to(k, s).wait_send()

        return carry

    lax.fori_loop(0, NS, sent, 0)
    for d in (1, 2, 3):
        for first in (k1, v1, q1):
            first(d).wait_send()
    for d, e in others:
        for then in (k2, v2, q2):
            then(d, e).wait_send()
    for p in range(NPAIR):
        for t in (1, 3):
            att0_to(p, t).wait_send()
            att0_on(p, t).wait_send()
    for t in range(1, NH):
        att1_to(t).wait_send()
    for b in range(2):
        for t in (1, 3):
            x3_to(b, t).wait_send()
            x3_on(b, t).wait_send()
        for t in range(NH):
            write(b, t).wait()


def shards(tokens, cluster_of, w_query, w_key, w_value, w_out):
    anywhere = pl.BlockSpec(memory_space=pl.ANY)
    return pl.pallas_call(
        kernel,
        out_shape=jax.ShapeDtypeStruct((ROWS, D), BF16),
        in_specs=[anywhere, pl.BlockSpec(memory_space=pltpu.VMEM)] + [anywhere] * 4,
        out_specs=anywhere,
        scratch_shapes=list(SCRATCH.values()),
        compiler_params=pltpu.CompilerParams(
            collective_id=0, has_side_effects=True, vmem_limit_bytes=VMEM_LIMIT
        ),
        name="three_layers",
    )(tokens, cluster_of.reshape(1, ROWS), w_query, w_key, w_value, w_out)


def solution(mesh):
    placed = (
        P("seq", None),
        P("seq"),
        P(None, "head", None),
        P(None, "head", None),
        P(None, "head", None),
        P(),
    )
    return jax.shard_map(
        shards, mesh=mesh, in_specs=placed, out_specs=P("seq", None), check_vma=False
    )
```

```python
import math
import types

import jax
import jax.numpy as jnp
from jax import lax
from jax.experimental import pallas as pl
from jax.experimental.pallas import tpu as pltpu
from jax.sharding import PartitionSpec as P

MESH = pl.DeviceIdType.MESH
D = 768
ROWS = 1024
HALF = 128
NS = 32
NH = 4
SLOTS = 64
PAIR = 256
NPAIR = ROWS // PAIR
LAST = NH - 1
FAR = -1e30
Q_SCALE = math.log2(math.e) / 8.0
VMEM_LIMIT = 60 * 1024 * 1024

NT = (((1,), (1,)), ((), ()))
NN = (((1,), (0,)), ((), ()))


def matmul(a, b, dims=NN):
    return lax.dot_general(a, b, dims, preferred_element_type=jnp.float32)


def lanes(shape):
    return lax.broadcasted_iota(jnp.int32, shape, 1)


def row_normed(rows):
    wide = rows.astype(jnp.float32)
    factor = lax.rsqrt(jnp.mean(wide * wide, axis=1, keepdims=True) + 1e-05)
    return (wide * factor).astype(jnp.bfloat16)


def only_head(rows, h):
    lane = lanes(rows.shape)
    keep = ((lane >= 64 * h) & (lane < 64 * h + 64)) | (lane >= 192)
    return jnp.where(keep, rows, jnp.zeros_like(rows))


def half_turn(rows):
    return pltpu.roll(rows, 64, 1)


def packed_third(third):
    m = third.shape[0] // 2
    return jnp.where(lanes((m, 128)) < 64, half_turn(third[:m]), third[m:])


NY, NX, NC = 4, 4, 2
GROUP = NX
NGROUP = NS // GROUP
GROWS = GROUP * SLOTS
ANSWER = SLOTS + SLOTS // 2
PACKED = PAIR + PAIR // 2

BF16, F32 = jnp.bfloat16, jnp.float32
DMA = pltpu.SemaphoreType.DMA
SCRATCH = {
    "x0": pltpu.VMEM((ROWS, D), BF16),
    "x1": pltpu.VMEM((ROWS, D), BF16),
    "x2": pltpu.VMEM((PAIR, D), BF16),
    "x3": pltpu.VMEM((ROWS, D), BF16),
    "w0": pltpu.VMEM((768, D), BF16),
    "w1": pltpu.VMEM((640, D), BF16),
    "w2": pltpu.VMEM((NH, 768, D), BF16),
    "wo": pltpu.VMEM((3, 768, D), BF16),
    "halo0": pltpu.VMEM((2, HALF, D), BF16),
    "halo2": pltpu.VMEM((2, HALF, D), BF16),
    "q0": pltpu.VMEM((ROWS, 256), BF16),
    "k0": pltpu.VMEM((ROWS + 2 * HALF, 256), BF16),
    "v0": pltpu.VMEM((ROWS + 2 * HALF, 256), BF16),
    "q2": pltpu.VMEM((NH, PAIR, 256), BF16),
    "k2": pltpu.VMEM((NH, PAIR + 2 * HALF, 256), BF16),
    "v2": pltpu.VMEM((NH, PAIR + 2 * HALF, 256), BF16),
    "att0": pltpu.VMEM((NH, NPAIR, PACKED, 128), BF16),
    "att1": pltpu.VMEM((NH, PACKED, 128), BF16),
    "own1": pltpu.VMEM((NPAIR, PACKED, 128), BF16),
    "chosen": pltpu.VMEM((NS * SLOTS, ROWS), BF16),
    "chosen_back": pltpu.VMEM((ROWS, NS * SLOTS), BF16),
    "within": pltpu.VMEM((ROWS, 128), F32),
    "packed": pltpu.VMEM((ROWS, 640), BF16),
    "out_k": pltpu.VMEM((NX, NY, NC, SLOTS, 256), BF16),
    "out_v": pltpu.VMEM((NY, NX, NC, SLOTS, 256), BF16),
    "out_q": pltpu.VMEM((NX, NY, NC, SLOTS, 128), BF16),
    "mid_k": pltpu.VMEM((NY, NC, NX, SLOTS, 256), BF16),
    "mid_v": pltpu.VMEM((NX, NC, NY, SLOTS, 256), BF16),
    "mid_q": pltpu.VMEM((NY, NC, NX, SLOTS, 128), BF16),
    "in_k": pltpu.VMEM((NY, NC, NX, SLOTS, 256), BF16),
    "in_v": pltpu.VMEM((NY, NC, NX, SLOTS, 256), BF16),
    "in_q": pltpu.VMEM((NY, NC, NX, SLOTS, 128), BF16),
    "q_third": pltpu.VMEM((NY, NC, NX, SLOTS, 128), BF16),
    "scores": pltpu.VMEM((3, GROWS, NS * SLOTS), F32),
    "answer": pltpu.VMEM((NS, ANSWER, 128), BF16),
    "back": pltpu.VMEM((NS, ANSWER, 128), BF16),
    "back_all": pltpu.VMEM((NS * SLOTS, 256), BF16),
    "x_sems": DMA((NPAIR,)),
    "w0_sems": DMA((4,)),
    "w1_sems": DMA((5,)),
    "w2_sems": DMA((4,)),
    "w2_send": DMA((NH, 3)),
    "w2_recv": DMA((NH, 3)),
    "w2_on_send": DMA((NH, 3)),
    "w2_on_recv": DMA((NH, 3)),
    "wo_sems": DMA((3, 2 * NH)),
    "halo0_send": DMA((2,)),
    "halo0_recv": DMA((2,)),
    "halo2_send": DMA((2,)),
    "halo2_recv": DMA((2,)),
    "att0_send": DMA((NPAIR, NH)),
    "att0_recv": DMA((NPAIR, NH)),
    "att1_send": DMA((NH,)),
    "att1_recv": DMA((NH,)),
    "k1_send": DMA((NX,)),
    "k1_recv": DMA((NX,)),
    "v1_send": DMA((NY,)),
    "v1_recv": DMA((NY,)),
    "q1_send": DMA((NX,)),
    "q1_recv": DMA((NX,)),
    "k2_send": DMA((NY, NC)),
    "k2_recv": DMA((NY, NC)),
    "v2_send": DMA((NX, NC)),
    "v2_recv": DMA((NX, NC)),
    "q2_send": DMA((NY, NC)),
    "q2_recv": DMA((NY, NC)),
    "a_send": DMA((NS,)),
    "a_recv": DMA((NS,)),
    "x3_send": DMA((2, NH)),
    "x3_recv": DMA((2, NH)),
    "out_sems": DMA((2, NH)),
}
N_ARGS = 7


def remote(src, dst, send_sem, recv_sem, device):
    return pltpu.make_async_remote_copy(
        src_ref=src,
        dst_ref=dst,
        send_sem=send_sem,
        recv_sem=recv_sem,
        device_id=device,
        device_id_type=MESH,
    )


def window_loads(source, target, sems):
    wq, wk, wv = source
    return [
        pltpu.make_async_copy(wq, target.at[pl.ds(0, 192)], sems.at[0]),
        pltpu.make_async_copy(wk, target.at[pl.ds(256, 192)], sems.at[1]),
        pltpu.make_async_copy(wv.at[pl.ds(0, 128)], target.at[pl.ds(512, 128)], sems.at[2]),
        pltpu.make_async_copy(wv.at[pl.ds(128, 64)], target.at[pl.ds(704, 64)], sems.at[3]),
    ]


def keep_keys(projected, k_rows, v_rows):
    k_rows[...] = projected[:, 0:256].astype(BF16)
    lane = lanes((projected.shape[0], 256))
    ones = (lane >= 128) & (lane < 192)
    v_rows[...] = jnp.where(ones, 1.0, projected[:, 256:512]).astype(BF16)


def window_block(queries, keys, values, place):
    query = lax.broadcasted_iota(jnp.int32, (HALF, 3 * HALF), 0)
    key = lax.broadcasted_iota(jnp.int32, (HALF, 3 * HALF), 1)
    allowed = (
        (key >= query)
        & (key < query + 2 * HALF)
        & (place + key >= 0)
        & (place + key < NS * ROWS)
    )
    bias = jnp.where(allowed, 0.0, FAR)
    stacked = jnp.concatenate([only_head(queries, g) for g in range(3)], axis=0)
    scores = matmul(stacked, keys, NT) + jnp.concatenate([bias] * 3, axis=0)
    highest = jnp.max(scores, axis=1, keepdims=True)
    weights = jnp.exp2(scores - highest).astype(BF16)
    sums = matmul(weights, values)
    scaled = sums * (1.0 / sums[:, 128:129])
    low = lanes((HALF, 128)) < 64
    first = jnp.where(low, scaled[0:HALF, 0:128], scaled[HALF : 2 * HALF, 0:128])
    return first, scaled[2 * HALF : 3 * HALF, 128:256]


def gathered_rows(blocks):
    half = PAIR // 2
    low = lanes((half, 128)) < 64
    parts = [block[0:PAIR] for block in blocks]
    for g in (0, 2):
        even = blocks[g][PAIR:PACKED].astype(F32)
        odd = blocks[g + 1][PAIR:PACKED].astype(F32)
        top = jnp.where(low, even, half_turn(odd))
        bottom = jnp.where(low, half_turn(even), odd)
        parts.append(jnp.concatenate([top, bottom], axis=0).astype(BF16))
    return jnp.concatenate(parts, axis=1)


def kernel(*refs):
    x_hbm, cluster, wq, wk, wv, w_out, out_hbm = refs[:N_ARGS]
    r = types.SimpleNamespace(**dict(zip(SCRATCH, refs[N_ARGS:])))
    s = lax.axis_index("seq")
    h = lax.axis_index("head")
    up, down = lax.rem(h + 1, NH), lax.rem(h + LAST, NH)
    right, left = lax.rem(s + 1, NS), lax.rem(s + NS - 1, NS)
    after = (lax.rem(s + (h + 1) // NH, NS), up)
    before = (lax.rem(s + NS - (LAST - h) // LAST, NS), down)

    barrier = pltpu.get_barrier_semaphore()

    def greet(i, carry):
        pl.semaphore_signal(barrier, 1, device_id=(lax.rem(s + i, NS), h), device_id_type=MESH)
        return carry

    lax.fori_loop(1, NS, greet, 0)
    for t in range(1, NH):
        pl.semaphore_signal(barrier, 1, device_id=(s, lax.rem(h + t, NH)), device_id_type=MESH)
    for near in (before, after):
        pl.semaphore_signal(barrier, 1, device_id=near, device_id_type=MESH)

    x_loads = [
        pltpu.make_async_copy(
            x_hbm.at[pl.ds(p * PAIR, PAIR)], r.x0.at[pl.ds(p * PAIR, PAIR)], r.x_sems.at[p]
        )
        for p in range(NPAIR)
    ]
    w0_loads = window_loads((wq.at[0], wk.at[0], wv.at[0]), r.w0, r.w0_sems)
    w1_loads = [
        pltpu.make_async_copy(src, r.w1.at[pl.ds(start, size)], r.w1_sems.at[i])
        for i, (src, start, size) in enumerate(
            [
                (wk.at[1], 0, 192),
                (wv.at[1, pl.ds(0, 128)], 256, 128),
                (wq.at[1, pl.ds(128, 64)], 384, 64),
                (wv.at[1, pl.ds(128, 64)], 448, 64),
                (wq.at[1, pl.ds(0, 128)], 512, 128),
            ]
        )
    ]
    w2_loads = window_loads((wq.at[2], wk.at[2], wv.at[2]), r.w2.at[h], r.w2_sems)
    wo_loads = [
        pltpu.make_async_copy(
            w_out.at[layer, pl.ds(192 * g + 128 * i, 128 - 64 * i)],
            r.wo.at[layer, pl.ds(128 * g + (512 - 64 * g) * i, 128 - 64 * i)],
            r.wo_sems.at[layer, 2 * g + i],
        )
        for layer in range(3)
        for g in range(NH)
        for i in range(2)
    ]
    for copy in x_loads + w0_loads:
        copy.start()
    r.w1[192:256, :] = jnp.zeros((64, D), BF16)
    for start in (192, 448, 640):
        r.w0[start : start + 64, :] = jnp.zeros((64, D), BF16)

    def clear(g, carry):
        for start in (192, 448, 640):
            r.w2[g, start : start + 64, :] = jnp.zeros((64, D), BF16)
        return carry

    lax.fori_loop(0, NH, clear, 0)
    for copy in x_loads:
        copy.wait()
    pl.semaphore_wait(barrier, NS - 1 + NH - 1 + 2)

    halos = [
        remote(
            r.x0.at[pl.ds(ROWS - HALF, HALF)],
            r.halo0.at[0],
            r.halo0_send.at[0],
            r.halo0_recv.at[0],
            (right, h),
        ),
        remote(
            r.x0.at[pl.ds(0, HALF)], r.halo0.at[1], r.halo0_send.at[1], r.halo0_recv.at[1], (left, h)
        ),
    ]
    for copy in halos:
        copy.start()
    for copy in w0_loads:
        copy.wait()
    for copy in w1_loads + wo_loads + w2_loads:
        copy.start()

    def project0(p, carry):
        rows = pl.ds(pl.multiple_of(p * PAIR, PAIR), PAIR)
        projected = matmul(row_normed(r.x0[rows, :]), r.w0[...], NT)
        r.q0[rows, :] = (projected[:, 0:256] * Q_SCALE).astype(BF16)
        inner = pl.ds(pl.multiple_of(p * PAIR + HALF, HALF), PAIR)
        keep_keys(projected[:, 256:768], r.k0.at[inner], r.v0.at[inner])
        return carry

    lax.fori_loop(0, NPAIR, project0, 0)

    def att0_to(p, t):
        block = r.att0.at[h, p]
        peer = (s, lax.rem(h + t, NH))
        return remote(block, block, r.att0_send.at[p, t], r.att0_recv.at[p, t], peer)

    def att0_on(p, t):
        half = PACKED // 2
        block = r.att0.at[lax.rem(h + NH - t, NH), p, pl.ds(half * (t // 2), half)]
        peer = (s, lax.rem(h + t, NH))
        return remote(block, block, r.att0_send.at[p, t - 1], r.att0_recv.at[p, t - 1], peer)

    def attend0(p, carry):
        firsts, thirds = [], []
        for b in range(2):
            begin = pl.multiple_of(p * PAIR + b * HALF, HALF)
            first, third = window_block(
                r.q0[pl.ds(begin, HALF), :],
                r.k0[pl.ds(begin, 3 * HALF), :],
                r.v0[pl.ds(begin, 3 * HALF), :],
                s * ROWS + begin - HALF,
            )
            firsts.append(first)
            thirds.append(third)
        r.att0[h, p, 0:PAIR, :] = jnp.concatenate(firsts, axis=0).astype(BF16)
        r.att0[h, p, PAIR:PACKED, :] = packed_third(jnp.concatenate(thirds, axis=0)).astype(BF16)
        for t in (1, 3):
            att0_to(p, t).start()
        return carry

    lax.fori_loop(1, NPAIR - 1, attend0, 0)
    for copy in halos:
        copy.wait()

    def edge0(side, carry):
        projected = matmul(row_normed(r.halo0[side]), r.w0[256:768, :], NT)
        outer = pl.ds(pl.multiple_of(side * (ROWS + HALF), HALF), HALF)
        keep_keys(projected, r.k0.at[outer], r.v0.at[outer])
        return attend0(side * (NPAIR - 1), carry)

    lax.fori_loop(0, 2, edge0, 0)

    def in_order(i):
        return lax.rem(i + 1, 3) + 2 * (i // 3)

    def hand_on(i):
        p = in_order(i)
        for t in (1, 3):
            att0_to(p, t).wait_recv()
        for t in (1, 3):
            att0_on(p, t).start()

    hand_on(0)

    ids = cluster[...]
    target = ids // 4
    mine = (target == lax.broadcasted_iota(jnp.int32, (NS, ROWS), 0)).astype(F32)
    earlier = (
        lax.broadcasted_iota(jnp.int32, (ROWS, ROWS), 0)
        < lax.broadcasted_iota(jnp.int32, (ROWS, ROWS), 1)
    ).astype(BF16)
    rank = jnp.sum(matmul(mine.astype(BF16), earlier) * mine, axis=0, keepdims=True)
    slot = target * SLOTS + rank.astype(jnp.int32)
    slot_col = jnp.transpose(jnp.broadcast_to(slot.astype(F32), (128, ROWS)))
    r.within[...] = jnp.transpose(
        jnp.broadcast_to((ids - 4 * target).astype(F32), (128, ROWS))
    )
    for p in range(NPAIR):
        col = jnp.concatenate([slot_col[p * PAIR : (p + 1) * PAIR]] * (NS * SLOTS // 128), axis=1)
        r.chosen_back[p * PAIR : (p + 1) * PAIR, :] = (
            col == lanes((PAIR, NS * SLOTS)).astype(F32)
        ).astype(BF16)

    hand_on(1)

    def choose(g, carry):
        rows = lax.broadcasted_iota(jnp.int32, (GROWS, ROWS), 0) + g * GROWS
        r.chosen[pl.ds(pl.multiple_of(g * GROWS, GROWS), GROWS), :] = (rows == slot).astype(BF16)
        return carry

    lax.fori_loop(0, NGROUP, choose, 0)
    hand_on(2)
    for copy in w1_loads + wo_loads:
        copy.wait()

    def finish0(i, carry):
        p = in_order(i)
        for t in (1, 3):
            att0_on(p, t).wait_recv()
        rows = pl.ds(pl.multiple_of(p * PAIR, PAIR), PAIR)
        gathered = gathered_rows([r.att0[g, p] for g in range(NH)])
        total = matmul(gathered, r.wo[0]) + r.x0[rows, :].astype(F32)
        x1 = total.astype(BF16)
        r.x1[rows, :] = x1
        projected = matmul(row_normed(x1), r.w1[...], NT)
        lane = lanes((PAIR, 128))
        mark = (r.within[rows, :] == (lane - 64).astype(F32)).astype(F32)
        scale = jnp.where(lane < 64, Q_SCALE, 1.0)
        r.packed[rows, 0:128] = projected[:, 0:128].astype(BF16)
        r.packed[rows, 128:256] = jnp.where(lane < 64, projected[:, 128:256], mark).astype(BF16)
        r.packed[rows, 256:384] = projected[:, 256:384].astype(BF16)
        r.packed[rows, 384:512] = (projected[:, 384:512] * scale).astype(BF16)
        r.packed[rows, 512:640] = (projected[:, 512:640] * Q_SCALE).astype(BF16)
        return carry

    lax.fori_loop(0, 1, finish0, 0)
    hand_on(3)
    lax.fori_loop(1, NPAIR, finish0, 0)

    y, x, c = s // (NX * NC), lax.rem(s // NC, NX), lax.rem(s, NC)

    def device(y_at, x_at, c_at):
        return (lax.rem(y_at, NY) * (NX * NC) + lax.rem(x_at, NX) * NC + lax.rem(c_at, NC), h)

    def along_x(out, mid, send, recv, d):
        column = lax.rem(x + d, NX)
        return remote(out.at[column], mid.at[:, :, x], send.at[d], recv.at[d], device(y, x + d, c))

    def along_y(out, mid, send, recv, d):
        row = lax.rem(y + d, NY)
        return remote(out.at[row], mid.at[:, :, y], send.at[d], recv.at[d], device(y + d, x, c))

    def k1(d):
        return along_x(r.out_k, r.mid_k, r.k1_send, r.k1_recv, d)

    def q1(d):
        return along_x(r.out_q, r.mid_q, r.q1_send, r.q1_recv, d)

    def v1(d):
        return along_y(r.out_v, r.mid_v, r.v1_send, r.v1_recv, d)

    def then_y(mid, into, send, recv, d, e):
        block = mid.at[lax.rem(y + d, NY), lax.rem(c + e, NC)]
        peer = device(y + d, x, c + e)
        return remote(block, into.at[y, c], send.at[d, e], recv.at[d, e], peer)

    def k2(d, e):
        return then_y(r.mid_k, r.in_k, r.k2_send, r.k2_recv, d, e)

    def q2(d, e):
        return then_y(r.mid_q, r.in_q, r.q2_send, r.q2_recv, d, e)

    def v2(d, e):
        block = r.mid_v.at[lax.rem(x + d, NX), lax.rem(c + e, NC)]
        peer = device(y, x + d, c + e)
        return remote(block, r.in_v.at[:, c, x], r.v2_send.at[d, e], r.v2_recv.at[d, e], peer)

    def answer_to(k, source):
        return remote(r.answer.at[k], r.back.at[source], r.a_send.at[k], r.a_recv.at[source], (k, h))

    def column_rows(column):
        return jnp.concatenate(
            [
                r.chosen[
                    pl.ds(pl.multiple_of((NX * n + column) * NC * SLOTS, NC * SLOTS), NC * SLOTS), :
                ]
                for n in range(NY)
            ],
            axis=0,
        )

    def pack(i, carry):
        d = lax.rem(i + 2, NX)
        column, row = lax.rem(x + d, NX), lax.rem(y + d, NY)
        keys = matmul(column_rows(column), r.packed[:, 0:256])
        lane = lanes(keys.shape)
        keys = jnp.where(lane < 192, keys, jnp.where(lane < 192 + 4, 1.0 - keys, 0.0))
        keys = keys.astype(BF16).reshape(NY, NC, SLOTS, 256)
        size = NX * NC * SLOTS
        rows = pl.ds(pl.multiple_of(row * size, size), size)
        values = matmul(r.chosen[rows, :], r.packed[:, 256:512])
        values = values.astype(BF16).reshape(NX, NC, SLOTS, 256)

        @pl.when(d != 0)
        def _():
            r.out_k[column] = keys
            k1(d).start()
            r.out_v[row] = values
            v1(d).start()

        @pl.when(d == 0)
        def _():
            for n in range(NY):
                for e in range(NC):
                    r.mid_k[n, e, x] = keys[n, e]
                    r.mid_v[n, e, y] = values[n, e]

        return carry

    lax.fori_loop(0, NX, pack, 0)

    for copy in w2_loads:
        copy.wait()
    pieces = ((512 * c, 128), (128 + 576 * c, 64), (256 + 96 * c, 96))
    twin = device(y, x, c + 1)

    def w2_to(t, i):
        start, size = pieces[i]
        block = r.w2.at[h, pl.ds(pl.multiple_of(start, 32), size)]
        peer = (s, lax.rem(h + t, NH))
        return remote(block, block, r.w2_send.at[t, i], r.w2_recv.at[t, i], peer)

    def w2_on(t, i):
        start, size = pieces[i]
        block = r.w2.at[lax.rem(h + NH - t, NH), pl.ds(pl.multiple_of(start, 32), size)]
        return remote(block, block, r.w2_on_send.at[t, i], r.w2_on_recv.at[t, i], twin)

    halves = [(t, i) for t in (2, 1, 3) for i in range(3)]
    for t, i in halves:
        w2_to(t, i).start()

    def pack_q(i, carry):
        d = lax.rem(i + 2, NX)
        column = lax.rem(x + d, NX)
        queries = matmul(column_rows(column), r.packed[:, 512:640])
        queries = queries.astype(BF16).reshape(NY, NC, SLOTS, 128)

        @pl.when(d != 0)
        def _():
            r.out_q[column] = queries

        @pl.when(d == 0)
        def _():
            for n in range(NY):
                for e in range(NC):
                    r.mid_q[n, e, x] = queries[n, e]

        return carry

    lax.fori_loop(0, NX, pack_q, 0)
    others = [(d, e) for d in (2, 1, 3, 0) for e in range(NC) if (d, e) != (0, 0)]
    for first, then in ((k1, k2), (v1, v2)):
        for d in (1, 2, 3):
            first(d).wait_recv()
        for d, e in others:
            then(d, e).start()

    for d in (2, 1, 3):
        q1(d).start()
    r.in_k[y, c] = r.mid_k[y, c]
    for n in range(NY):
        r.in_v[n, c, x] = r.mid_v[x, c, n]
    for then in (k2, v2):
        for d, e in others:
            then(d, e).wait_recv()

    for t, i in halves:
        w2_to(t, i).wait_recv()
        w2_on(t, i).start()

    def settle(g, carry):
        at = (g // NC, lax.rem(g, NC))
        lane = lax.broadcasted_iota(jnp.int32, (NX, SLOTS, 128), 2)
        other = r.in_k[(*at, slice(None), slice(None), slice(128, 256))].astype(F32)
        third = r.in_v[(*at, slice(None), slice(None), slice(128, 256))]
        marks = jnp.where(lane < 68, FAR * (1.0 - other), 0.0)
        r.q_third[at] = jnp.where(lane < 64, third.astype(F32), marks).astype(BF16)
        r.in_v[(*at, slice(None), slice(None), slice(128, 256))] = jnp.where(
            lane < 64, jnp.ones_like(third), third
        )
        return carry

    lax.fori_loop(0, NGROUP, settle, 0)
    for d in (1, 2, 3):
        q1(d).wait_recv()
    for d, e in ((0, 1), (3, 0), (3, 1), (2, 0), (2, 1), (1, 0), (1, 1)):
        q2(d, e).start()
    r.in_q[y, c] = r.mid_q[y, c]

    def group(i):
        return lax.rem(y + i // NC, NY) * NC + lax.rem(c + i, NC)

    def score(i, head):
        g = group(i)
        at = (g // NC, lax.rem(g, NC))
        queries = jnp.concatenate(
            [r.in_q[at].reshape(GROWS, 128), r.q_third[at].reshape(GROWS, 128)], axis=1
        )
        keys = r.in_k[...].reshape(NS * SLOTS, 256)
        r.scores[head] = matmul(only_head(queries, head), keys, NT)

    def weigh(head):
        scores = r.scores[head]
        highest = jnp.max(scores, axis=1, keepdims=True)
        weights = jnp.exp2(scores - highest).astype(BF16)
        sums = matmul(weights, r.in_v[...].reshape(NS * SLOTS, 256))
        return sums * (1.0 / sums[:, 128:129])

    score(0, 0)

    def attend1(i, carry, last=False):
        g = group(i)
        if not last:
            q2(lax.rem(NY - (i + 1) // NC, NY), lax.rem(i + 1, NC)).wait_recv()
        scaled = []
        for head in range(3):
            if not (last and head == 2):
                score(i + (head + 1) // 3, (head + 1) % 3)
            scaled.append(weigh(head))
        firsts = jnp.where(lanes((GROWS, 128)) < 64, scaled[0][:, 0:128], scaled[1][:, 0:128])
        third = scaled[2][:, 128:256]
        for j in range(GROUP):
            k = (g // NC) * (NX * NC) + j * NC + lax.rem(g, NC)
            rows = slice(j * SLOTS, (j + 1) * SLOTS)
            a_part = firsts[rows].astype(BF16)
            b_part = packed_third(third[rows]).astype(BF16)
            r.answer[k, 0:SLOTS, :] = a_part
            r.answer[k, SLOTS:ANSWER, :] = b_part

            @pl.when(k != s)
            def _():
                answer_to(k, s).start()

            @pl.when(k == s)
            def _():
                r.back[k, 0:SLOTS, :] = a_part
                r.back[k, SLOTS:ANSWER, :] = b_part

        return carry

    lax.fori_loop(0, NGROUP - 1, attend1, 0)
    attend1(NGROUP - 1, 0, last=True)

    def arrive_back(g, carry):
        for j in range(4):
            k = 4 * g + j

            @pl.when(k != s)
            def _():
                answer_to(k, k).wait_recv()

        block = r.back[pl.ds(4 * g, 4)]
        rows = pl.ds(pl.multiple_of(g * PAIR, PAIR), PAIR)
        third = block[:, SLOTS:ANSWER, :]
        turned = half_turn(third.astype(F32).reshape(HALF, 128)).astype(BF16)
        turned = turned.reshape(4, SLOTS // 2, 128)
        r.back_all[rows, 0:128] = block[:, 0:SLOTS, :].reshape(PAIR, 128)
        r.back_all[rows, 128:256] = jnp.concatenate([turned, third], axis=1).reshape(PAIR, 128)
        return carry

    lax.fori_loop(0, NS // 4, arrive_back, 0)

    def att1_to(t):
        peer = lax.rem(h + t, NH)
        return remote(r.own1.at[peer], r.att1.at[h], r.att1_send.at[t], r.att1_recv.at[t], (s, peer))

    def att1_from(t):
        source = lax.rem(h + NH - t, NH)
        return remote(
            r.own1.at[source], r.att1.at[source], r.att1_send.at[t], r.att1_recv.at[t], (s, source)
        )

    def unpack(t):
        p = lax.rem(h + t, NH)
        rows = pl.ds(pl.multiple_of(p * PAIR, PAIR), PAIR)
        own = matmul(r.chosen_back[rows, :], r.back_all[...])
        return p, own[:, 0:128].astype(BF16), packed_third(own[:, 128:256]).astype(BF16)

    for t in (2, 1, 3):
        p, first, third = unpack(t)
        r.own1[p, 0:PAIR, :] = first
        r.own1[p, PAIR:PACKED, :] = third
        att1_to(t).start()
    _, first, third = unpack(0)
    r.att1[h, 0:PAIR, :] = first
    r.att1[h, PAIR:PACKED, :] = third
    for t in range(1, NH):
        att1_from(t).wait_recv()
    quarter = pl.ds(pl.multiple_of(h * PAIR, PAIR), PAIR)
    total = matmul(gathered_rows([r.att1[g] for g in range(NH)]), r.wo[1])
    r.x2[...] = (total + r.x1[quarter, :].astype(F32)).astype(BF16)

    halos2 = [
        remote(
            r.x2.at[pl.ds(PAIR - HALF, HALF)],
            r.halo2.at[0],
            r.halo2_send.at[0],
            r.halo2_recv.at[0],
            after,
        ),
        remote(
            r.x2.at[pl.ds(0, HALF)], r.halo2.at[1], r.halo2_send.at[1], r.halo2_recv.at[1], before
        ),
    ]
    for copy in halos2:
        copy.start()
    for t, i in halves:
        w2_on(t, i).wait_recv()
    normed = row_normed(r.x2[...])
    inner = pl.ds(HALF, PAIR)
    for g in range(NH):
        projected = matmul(normed, r.w2[g], NT)
        r.q2[g] = (projected[:, 0:256] * Q_SCALE).astype(BF16)
        keep_keys(projected[:, 256:768], r.k2.at[g, inner], r.v2.at[g, inner])
    for copy in halos2:
        copy.wait()
    normed = row_normed(r.halo2[...].reshape(2 * HALF, D))
    for g in range(NH):
        projected = matmul(normed, r.w2[g, 256:768, :], NT)
        for side in range(2):
            outer = pl.ds(side * (PAIR + HALF), HALF)
            keep_keys(
                projected[side * HALF : (side + 1) * HALF], r.k2.at[g, outer], r.v2.at[g, outer]
            )

    def x3_to(b, t):
        block = r.x3.at[pl.ds(pl.multiple_of(h * PAIR + b * HALF, HALF), HALF)]
        peer = (s, lax.rem(h + t, NH))
        return remote(block, block, r.x3_send.at[b, t], r.x3_recv.at[b, t], peer)

    def x3_on(b, t):
        source = lax.rem(h + NH - t, NH)
        half = HALF // 2
        block = r.x3.at[
            pl.ds(pl.multiple_of(source * PAIR + b * HALF + half * (t // 2), half), half)
        ]
        peer = (s, lax.rem(h + t, NH))
        return remote(block, block, r.x3_send.at[b, t - 1], r.x3_recv.at[b, t - 1], peer)

    def write(b, t):
        rows = pl.ds(pl.multiple_of(lax.rem(h + t, NH) * PAIR + b * HALF, HALF), HALF)
        return pltpu.make_async_copy(r.x3.at[rows], out_hbm.at[rows], r.out_sems.at[b, t])

    for b in range(2):
        begin = b * HALF
        firsts, thirds = [], []
        for g in range(NH):
            first, third = window_block(
                r.q2[g, begin : begin + HALF, :],
                r.k2[g, begin : begin + 3 * HALF, :],
                r.v2[g, begin : begin + 3 * HALF, :],
                s * ROWS + h * PAIR + begin - HALF,
            )
            firsts.append(first)
            thirds.append(third)
        low = lanes((HALF, 128)) < 64
        for g in (0, 2):
            firsts.append(jnp.where(low, half_turn(thirds[g]), thirds[g + 1]))
        gathered = jnp.concatenate([first.astype(BF16) for first in firsts], axis=1)
        total = matmul(gathered, r.wo[2]) + r.x2[begin : begin + HALF, :].astype(F32)
        rows = pl.ds(pl.multiple_of(h * PAIR + begin, HALF), HALF)
        r.x3[rows, :] = total.astype(BF16)
        for t in (1, 3):
            x3_to(b, t).start()
        write(b, 0).start()
    for b in range(2):
        for t in (1, 3):
            x3_to(b, t).wait_recv()
        for t in (1, 3):
            x3_on(b, t).start()
        for t in (1, 3):
            write(b, t).start()
    for b in range(2):
        for t in (1, 3):
            x3_on(b, t).wait_recv()
        write(b, 2).start()

    def sent(k, carry):
        @pl.when(k != s)
        def _():
            answer_to(k, s).wait_send()

        return carry

    lax.fori_loop(0, NS, sent, 0)
    for t, i in halves:
        w2_to(t, i).wait_send()
        w2_on(t, i).wait_send()
    for d in (1, 2, 3):
        for first in (k1, v1, q1):
            first(d).wait_send()
    for d, e in others:
        for then in (k2, v2, q2):
            then(d, e).wait_send()
    for p in range(NPAIR):
        for t in (1, 3):
            att0_to(p, t).wait_send()
            att0_on(p, t).wait_send()
    for t in range(1, NH):
        att1_to(t).wait_send()
    for b in range(2):
        for t in (1, 3):
            x3_to(b, t).wait_send()
            x3_on(b, t).wait_send()
        for t in range(NH):
            write(b, t).wait()


def shards(tokens, cluster_of, w_query, w_key, w_value, w_out):
    anywhere = pl.BlockSpec(memory_space=pl.ANY)
    return pl.pallas_call(
        kernel,
        out_shape=jax.ShapeDtypeStruct((ROWS, D), BF16),
        in_specs=[anywhere, pl.BlockSpec(memory_space=pltpu.VMEM)] + [anywhere] * 4,
        out_specs=anywhere,
        scratch_shapes=list(SCRATCH.values()),
        compiler_params=pltpu.CompilerParams(
            collective_id=0, has_side_effects=True, vmem_limit_bytes=VMEM_LIMIT
        ),
        name="three_layers",
    )(tokens, cluster_of.reshape(1, ROWS), w_query, w_key, w_value, w_out)


def solution(mesh):
    placed = (
        P("seq", None),
        P("seq"),
        P(None, "head", None),
        P(None, "head", None),
        P(None, "head", None),
        P(),
    )
    return jax.shard_map(
        shards, mesh=mesh, in_specs=placed, out_specs=P("seq", None), check_vma=False
    )
```

```python
import math
import types

import jax
import jax.numpy as jnp
from jax import lax
from jax.experimental import pallas as pl
from jax.experimental.pallas import tpu as pltpu
from jax.sharding import PartitionSpec as P

MESH = pl.DeviceIdType.MESH
D = 768
ROWS = 1024
HALF = 128
NS = 32
NH = 4
SLOTS = 64
PAIR = 256
NPAIR = ROWS // PAIR
LAST = NH - 1
FAR = -1e30
Q_SCALE = math.log2(math.e) / 8.0
VMEM_LIMIT = 60 * 1024 * 1024

NT = (((1,), (1,)), ((), ()))
NN = (((1,), (0,)), ((), ()))


def matmul(a, b, dims=NN):
    return lax.dot_general(a, b, dims, preferred_element_type=jnp.float32)


def lanes(shape):
    return lax.broadcasted_iota(jnp.int32, shape, 1)


def row_normed(rows):
    wide = rows.astype(jnp.float32)
    factor = lax.rsqrt(jnp.mean(wide * wide, axis=1, keepdims=True) + 1e-05)
    return (wide * factor).astype(jnp.bfloat16)


def only_head(rows, h):
    lane = lanes(rows.shape)
    keep = ((lane >= 64 * h) & (lane < 64 * h + 64)) | (lane >= 192)
    return jnp.where(keep, rows, jnp.zeros_like(rows))


def half_turn(rows):
    return pltpu.roll(rows, 64, 1)


def packed_third(third):
    m = third.shape[0] // 2
    return jnp.where(lanes((m, 128)) < 64, half_turn(third[:m]), third[m:])


NY, NX, NC = 4, 4, 2
GROUP = NX
NGROUP = NS // GROUP
GROWS = GROUP * SLOTS
ANSWER = SLOTS + SLOTS // 2
PACKED = PAIR + PAIR // 2

BF16, F32 = jnp.bfloat16, jnp.float32
DMA = pltpu.SemaphoreType.DMA
SCRATCH = {
    "x0": pltpu.VMEM((ROWS, D), BF16),
    "x1": pltpu.VMEM((ROWS, D), BF16),
    "x2": pltpu.VMEM((PAIR, D), BF16),
    "x3": pltpu.VMEM((ROWS, D), BF16),
    "w0": pltpu.VMEM((768, D), BF16),
    "w1": pltpu.VMEM((640, D), BF16),
    "w2": pltpu.VMEM((NH, 768, D), BF16),
    "wo": pltpu.VMEM((3, 768, D), BF16),
    "halo0": pltpu.VMEM((2, HALF, D), BF16),
    "halo2": pltpu.VMEM((2, HALF, D), BF16),
    "q0": pltpu.VMEM((ROWS, 256), BF16),
    "k0": pltpu.VMEM((ROWS + 2 * HALF, 256), BF16),
    "v0": pltpu.VMEM((ROWS + 2 * HALF, 256), BF16),
    "q2": pltpu.VMEM((NH, PAIR, 256), BF16),
    "k2": pltpu.VMEM((NH, PAIR + 2 * HALF, 256), BF16),
    "v2": pltpu.VMEM((NH, PAIR + 2 * HALF, 256), BF16),
    "att0": pltpu.VMEM((NH, NPAIR, PACKED, 128), BF16),
    "att1": pltpu.VMEM((NH, PACKED, 128), BF16),
    "own1": pltpu.VMEM((NPAIR, PACKED, 128), BF16),
    "chosen": pltpu.VMEM((NS * SLOTS, ROWS), BF16),
    "chosen_back": pltpu.VMEM((ROWS, NS * SLOTS), BF16),
    "within": pltpu.VMEM((ROWS, 128), F32),
    "packed": pltpu.VMEM((ROWS, 640), BF16),
    "out_k": pltpu.VMEM((NX, NY, NC, SLOTS, 256), BF16),
    "out_v": pltpu.VMEM((NY, NX, NC, SLOTS, 256), BF16),
    "out_q": pltpu.VMEM((NX, NY, NC, SLOTS, 128), BF16),
    "mid_k": pltpu.VMEM((NY, NC, NX, SLOTS, 256), BF16),
    "mid_v": pltpu.VMEM((NX, NC, NY, SLOTS, 256), BF16),
    "mid_q": pltpu.VMEM((NY, NC, NX, SLOTS, 128), BF16),
    "in_k": pltpu.VMEM((NY, NC, NX, SLOTS, 256), BF16),
    "in_v": pltpu.VMEM((NY, NC, NX, SLOTS, 256), BF16),
    "in_q": pltpu.VMEM((NY, NC, NX, SLOTS, 128), BF16),
    "q_third": pltpu.VMEM((NY, NC, NX, SLOTS, 128), BF16),
    "scores": pltpu.VMEM((3, GROWS, NS * SLOTS), F32),
    "answer": pltpu.VMEM((NS, ANSWER, 128), BF16),
    "back": pltpu.VMEM((NS, ANSWER, 128), BF16),
    "back_all": pltpu.VMEM((NS * SLOTS, 256), BF16),
    "x_sems": DMA((NPAIR,)),
    "w0_sems": DMA((4,)),
    "w1_sems": DMA((5,)),
    "w2_sems": DMA((4,)),
    "w2_send": DMA((NH, 3)),
    "w2_recv": DMA((NH, 3)),
    "w2_on_send": DMA((NH, 3)),
    "w2_on_recv": DMA((NH, 3)),
    "wo_sems": DMA((3, 2 * NH)),
    "halo0_send": DMA((2,)),
    "halo0_recv": DMA((2,)),
    "halo2_send": DMA((2,)),
    "halo2_recv": DMA((2,)),
    "att0_send": DMA((NPAIR, NH)),
    "att0_recv": DMA((NPAIR, NH)),
    "att1_send": DMA((NH,)),
    "att1_recv": DMA((NH,)),
    "k1_send": DMA((NX,)),
    "k1_recv": DMA((NX,)),
    "v1_send": DMA((NY,)),
    "v1_recv": DMA((NY,)),
    "q1_send": DMA((NX,)),
    "q1_recv": DMA((NX,)),
    "k2_send": DMA((NY, NC)),
    "k2_recv": DMA((NY, NC)),
    "v2_send": DMA((NX, NC)),
    "v2_recv": DMA((NX, NC)),
    "q2_send": DMA((NY, NC)),
    "q2_recv": DMA((NY, NC)),
    "a_send": DMA((NS,)),
    "a_recv": DMA((NS,)),
    "x3_send": DMA((2, NH)),
    "x3_recv": DMA((2, NH)),
    "out_sems": DMA((2, NH)),
}
N_ARGS = 7


def remote(src, dst, send_sem, recv_sem, device):
    return pltpu.make_async_remote_copy(
        src_ref=src,
        dst_ref=dst,
        send_sem=send_sem,
        recv_sem=recv_sem,
        device_id=device,
        device_id_type=MESH,
    )


def window_loads(source, target, sems):
    wq, wk, wv = source
    return [
        pltpu.make_async_copy(wq, target.at[pl.ds(0, 192)], sems.at[0]),
        pltpu.make_async_copy(wk, target.at[pl.ds(256, 192)], sems.at[1]),
        pltpu.make_async_copy(wv.at[pl.ds(0, 128)], target.at[pl.ds(512, 128)], sems.at[2]),
        pltpu.make_async_copy(wv.at[pl.ds(128, 64)], target.at[pl.ds(704, 64)], sems.at[3]),
    ]


def keep_keys(projected, k_rows, v_rows):
    k_rows[...] = projected[:, 0:256].astype(BF16)
    lane = lanes((projected.shape[0], 256))
    ones = (lane >= 128) & (lane < 192)
    v_rows[...] = jnp.where(ones, 1.0, projected[:, 256:512]).astype(BF16)


def window_block(queries, keys, values, place):
    query = lax.broadcasted_iota(jnp.int32, (HALF, 3 * HALF), 0)
    key = lax.broadcasted_iota(jnp.int32, (HALF, 3 * HALF), 1)
    allowed = (
        (key >= query)
        & (key < query + 2 * HALF)
        & (place + key >= 0)
        & (place + key < NS * ROWS)
    )
    bias = jnp.where(allowed, 0.0, FAR)
    stacked = jnp.concatenate([only_head(queries, g) for g in range(3)], axis=0)
    scores = matmul(stacked, keys, NT) + jnp.concatenate([bias] * 3, axis=0)
    highest = jnp.max(scores, axis=1, keepdims=True)
    weights = jnp.exp2(scores - highest).astype(BF16)
    sums = matmul(weights, values)
    scaled = sums * (1.0 / sums[:, 128:129])
    low = lanes((HALF, 128)) < 64
    first = jnp.where(low, scaled[0:HALF, 0:128], scaled[HALF : 2 * HALF, 0:128])
    return first, scaled[2 * HALF : 3 * HALF, 128:256]


def gathered_rows(blocks):
    half = PAIR // 2
    low = lanes((half, 128)) < 64
    parts = [block[0:PAIR] for block in blocks]
    for g in (0, 2):
        even = blocks[g][PAIR:PACKED].astype(F32)
        odd = blocks[g + 1][PAIR:PACKED].astype(F32)
        top = jnp.where(low, even, half_turn(odd))
        bottom = jnp.where(low, half_turn(even), odd)
        parts.append(jnp.concatenate([top, bottom], axis=0).astype(BF16))
    return jnp.concatenate(parts, axis=1)


def kernel(*refs):
    x_hbm, cluster, wq, wk, wv, w_out, out_hbm = refs[:N_ARGS]
    r = types.SimpleNamespace(**dict(zip(SCRATCH, refs[N_ARGS:])))
    s = lax.axis_index("seq")
    h = lax.axis_index("head")
    up, down = lax.rem(h + 1, NH), lax.rem(h + LAST, NH)
    right, left = lax.rem(s + 1, NS), lax.rem(s + NS - 1, NS)
    after = (lax.rem(s + (h + 1) // NH, NS), up)
    before = (lax.rem(s + NS - (LAST - h) // LAST, NS), down)

    barrier = pltpu.get_barrier_semaphore()

    def greet(i, carry):
        pl.semaphore_signal(barrier, 1, device_id=(lax.rem(s + i, NS), h), device_id_type=MESH)
        return carry

    lax.fori_loop(1, NS, greet, 0)
    for t in range(1, NH):
        pl.semaphore_signal(barrier, 1, device_id=(s, lax.rem(h + t, NH)), device_id_type=MESH)
    for near in (before, after):
        pl.semaphore_signal(barrier, 1, device_id=near, device_id_type=MESH)

    x_loads = [
        pltpu.make_async_copy(
            x_hbm.at[pl.ds(p * PAIR, PAIR)], r.x0.at[pl.ds(p * PAIR, PAIR)], r.x_sems.at[p]
        )
        for p in range(NPAIR)
    ]
    w0_loads = window_loads((wq.at[0], wk.at[0], wv.at[0]), r.w0, r.w0_sems)
    w1_loads = [
        pltpu.make_async_copy(src, r.w1.at[pl.ds(start, size)], r.w1_sems.at[i])
        for i, (src, start, size) in enumerate(
            [
                (wk.at[1], 0, 192),
                (wv.at[1, pl.ds(0, 128)], 256, 128),
                (wq.at[1, pl.ds(128, 64)], 384, 64),
                (wv.at[1, pl.ds(128, 64)], 448, 64),
                (wq.at[1, pl.ds(0, 128)], 512, 128),
            ]
        )
    ]
    w2_loads = window_loads((wq.at[2], wk.at[2], wv.at[2]), r.w2.at[h], r.w2_sems)
    wo_loads = [
        pltpu.make_async_copy(
            w_out.at[layer, pl.ds(192 * g + 128 * i, 128 - 64 * i)],
            r.wo.at[layer, pl.ds(128 * g + (512 - 64 * g) * i, 128 - 64 * i)],
            r.wo_sems.at[layer, 2 * g + i],
        )
        for layer in range(3)
        for g in range(NH)
        for i in range(2)
    ]
    for copy in x_loads + w0_loads:
        copy.start()
    r.w1[192:256, :] = jnp.zeros((64, D), BF16)
    for start in (192, 448, 640):
        r.w0[start : start + 64, :] = jnp.zeros((64, D), BF16)

    def clear(g, carry):
        for start in (192, 448, 640):
            r.w2[g, start : start + 64, :] = jnp.zeros((64, D), BF16)
        return carry

    lax.fori_loop(0, NH, clear, 0)
    for copy in x_loads:
        copy.wait()
    pl.semaphore_wait(barrier, NS - 1 + NH - 1 + 2)

    halos = [
        remote(
            r.x0.at[pl.ds(ROWS - HALF, HALF)],
            r.halo0.at[0],
            r.halo0_send.at[0],
            r.halo0_recv.at[0],
            (right, h),
        ),
        remote(
            r.x0.at[pl.ds(0, HALF)], r.halo0.at[1], r.halo0_send.at[1], r.halo0_recv.at[1], (left, h)
        ),
    ]
    for copy in halos:
        copy.start()
    for copy in w0_loads:
        copy.wait()
    for copy in w1_loads + wo_loads + w2_loads:
        copy.start()

    def project0(p, carry):
        rows = pl.ds(pl.multiple_of(p * PAIR, PAIR), PAIR)
        projected = matmul(row_normed(r.x0[rows, :]), r.w0[...], NT)
        r.q0[rows, :] = (projected[:, 0:256] * Q_SCALE).astype(BF16)
        inner = pl.ds(pl.multiple_of(p * PAIR + HALF, HALF), PAIR)
        keep_keys(projected[:, 256:768], r.k0.at[inner], r.v0.at[inner])
        return carry

    lax.fori_loop(0, NPAIR, project0, 0)

    def att0_to(p, t):
        block = r.att0.at[h, p]
        peer = (s, lax.rem(h + t, NH))
        return remote(block, block, r.att0_send.at[p, t], r.att0_recv.at[p, t], peer)

    def att0_on(p, t):
        half = PACKED // 2
        block = r.att0.at[lax.rem(h + NH - t, NH), p, pl.ds(half * (t // 2), half)]
        peer = (s, lax.rem(h + t, NH))
        return remote(block, block, r.att0_send.at[p, t - 1], r.att0_recv.at[p, t - 1], peer)

    def attend0(p, carry):
        firsts, thirds = [], []
        for b in range(2):
            begin = pl.multiple_of(p * PAIR + b * HALF, HALF)
            first, third = window_block(
                r.q0[pl.ds(begin, HALF), :],
                r.k0[pl.ds(begin, 3 * HALF), :],
                r.v0[pl.ds(begin, 3 * HALF), :],
                s * ROWS + begin - HALF,
            )
            firsts.append(first)
            thirds.append(third)
        r.att0[h, p, 0:PAIR, :] = jnp.concatenate(firsts, axis=0).astype(BF16)
        r.att0[h, p, PAIR:PACKED, :] = packed_third(jnp.concatenate(thirds, axis=0)).astype(BF16)
        for t in (1, 3):
            att0_to(p, t).start()
        return carry

    lax.fori_loop(1, NPAIR - 1, attend0, 0)
    for copy in halos:
        copy.wait()

    def edge0(side, carry):
        projected = matmul(row_normed(r.halo0[side]), r.w0[256:768, :], NT)
        outer = pl.ds(pl.multiple_of(side * (ROWS + HALF), HALF), HALF)
        keep_keys(projected, r.k0.at[outer], r.v0.at[outer])
        return attend0(side * (NPAIR - 1), carry)

    lax.fori_loop(0, 2, edge0, 0)

    def in_order(i):
        return lax.rem(i + 1, 3) + 2 * (i // 3)

    def hand_on(i):
        p = in_order(i)
        for t in (1, 3):
            att0_to(p, t).wait_recv()
        for t in (1, 3):
            att0_on(p, t).start()

    hand_on(0)

    ids = cluster[...]
    target = ids // 4
    mine = (target == lax.broadcasted_iota(jnp.int32, (NS, ROWS), 0)).astype(F32)
    earlier = (
        lax.broadcasted_iota(jnp.int32, (ROWS, ROWS), 0)
        < lax.broadcasted_iota(jnp.int32, (ROWS, ROWS), 1)
    ).astype(BF16)
    rank = jnp.sum(matmul(mine.astype(BF16), earlier) * mine, axis=0, keepdims=True)
    slot = target * SLOTS + rank.astype(jnp.int32)
    slot_col = jnp.transpose(jnp.broadcast_to(slot.astype(F32), (128, ROWS)))
    r.within[...] = jnp.transpose(
        jnp.broadcast_to((ids - 4 * target).astype(F32), (128, ROWS))
    )
    for p in range(NPAIR):
        col = jnp.concatenate([slot_col[p * PAIR : (p + 1) * PAIR]] * (NS * SLOTS // 128), axis=1)
        r.chosen_back[p * PAIR : (p + 1) * PAIR, :] = (
            col == lanes((PAIR, NS * SLOTS)).astype(F32)
        ).astype(BF16)

    hand_on(1)

    def choose(g, carry):
        rows = lax.broadcasted_iota(jnp.int32, (GROWS, ROWS), 0) + g * GROWS
        r.chosen[pl.ds(pl.multiple_of(g * GROWS, GROWS), GROWS), :] = (rows == slot).astype(BF16)
        return carry

    lax.fori_loop(0, NGROUP, choose, 0)
    hand_on(2)
    for copy in w1_loads + wo_loads:
        copy.wait()

    def finish0(i, carry):
        p = in_order(i)
        for t in (1, 3):
            att0_on(p, t).wait_recv()
        rows = pl.ds(pl.multiple_of(p * PAIR, PAIR), PAIR)
        gathered = gathered_rows([r.att0[g, p] for g in range(NH)])
        total = matmul(gathered, r.wo[0]) + r.x0[rows, :].astype(F32)
        x1 = total.astype(BF16)
        r.x1[rows, :] = x1
        projected = matmul(row_normed(x1), r.w1[...], NT)
        lane = lanes((PAIR, 128))
        mark = (r.within[rows, :] == (lane - 64).astype(F32)).astype(F32)
        scale = jnp.where(lane < 64, Q_SCALE, 1.0)
        r.packed[rows, 0:128] = projected[:, 0:128].astype(BF16)
        r.packed[rows, 128:256] = jnp.where(lane < 64, projected[:, 128:256], mark).astype(BF16)
        r.packed[rows, 256:384] = projected[:, 256:384].astype(BF16)
        r.packed[rows, 384:512] = (projected[:, 384:512] * scale).astype(BF16)
        r.packed[rows, 512:640] = (projected[:, 512:640] * Q_SCALE).astype(BF16)
        return carry

    lax.fori_loop(0, 1, finish0, 0)
    hand_on(3)
    lax.fori_loop(1, NPAIR, finish0, 0)

    y, x, c = s // (NX * NC), lax.rem(s // NC, NX), lax.rem(s, NC)

    def device(y_at, x_at, c_at):
        return (lax.rem(y_at, NY) * (NX * NC) + lax.rem(x_at, NX) * NC + lax.rem(c_at, NC), h)

    def along_x(out, mid, send, recv, d):
        column = lax.rem(x + d, NX)
        return remote(out.at[column], mid.at[:, :, x], send.at[d], recv.at[d], device(y, x + d, c))

    def along_y(out, mid, send, recv, d):
        row = lax.rem(y + d, NY)
        return remote(out.at[row], mid.at[:, :, y], send.at[d], recv.at[d], device(y + d, x, c))

    def k1(d):
        return along_x(r.out_k, r.mid_k, r.k1_send, r.k1_recv, d)

    def q1(d):
        return along_x(r.out_q, r.mid_q, r.q1_send, r.q1_recv, d)

    def v1(d):
        return along_y(r.out_v, r.mid_v, r.v1_send, r.v1_recv, d)

    def then_y(mid, into, send, recv, d, e):
        block = mid.at[lax.rem(y + d, NY), lax.rem(c + e, NC)]
        peer = device(y + d, x, c + e)
        return remote(block, into.at[y, c], send.at[d, e], recv.at[d, e], peer)

    def k2(d, e):
        return then_y(r.mid_k, r.in_k, r.k2_send, r.k2_recv, d, e)

    def q2(d, e):
        return then_y(r.mid_q, r.in_q, r.q2_send, r.q2_recv, d, e)

    def v2(d, e):
        block = r.mid_v.at[lax.rem(x + d, NX), lax.rem(c + e, NC)]
        peer = device(y, x + d, c + e)
        return remote(block, r.in_v.at[:, c, x], r.v2_send.at[d, e], r.v2_recv.at[d, e], peer)

    def answer_to(k, source):
        return remote(r.answer.at[k], r.back.at[source], r.a_send.at[k], r.a_recv.at[source], (k, h))

    def column_rows(column):
        return jnp.concatenate(
            [
                r.chosen[
                    pl.ds(pl.multiple_of((NX * n + column) * NC * SLOTS, NC * SLOTS), NC * SLOTS), :
                ]
                for n in range(NY)
            ],
            axis=0,
        )

    def pack(i, carry):
        d = lax.rem(i + 2, NX)
        column, row = lax.rem(x + d, NX), lax.rem(y + d, NY)
        keys = matmul(column_rows(column), r.packed[:, 0:256])
        lane = lanes(keys.shape)
        keys = jnp.where(lane < 192, keys, jnp.where(lane < 192 + 4, 1.0 - keys, 0.0))
        keys = keys.astype(BF16).reshape(NY, NC, SLOTS, 256)
        size = NX * NC * SLOTS
        rows = pl.ds(pl.multiple_of(row * size, size), size)
        values = matmul(r.chosen[rows, :], r.packed[:, 256:512])
        values = values.astype(BF16).reshape(NX, NC, SLOTS, 256)

        @pl.when(d != 0)
        def _():
            r.out_k[column] = keys
            k1(d).start()
            r.out_v[row] = values
            v1(d).start()

        @pl.when(d == 0)
        def _():
            for n in range(NY):
                for e in range(NC):
                    r.mid_k[n, e, x] = keys[n, e]
                    r.mid_v[n, e, y] = values[n, e]

        return carry

    lax.fori_loop(0, NX, pack, 0)

    for copy in w2_loads:
        copy.wait()
    pieces = ((512 * c, 128), (128 + 576 * c, 64), (256 + 96 * c, 96))
    twin = device(y, x, c + 1)

    def w2_to(t, i):
        start, size = pieces[i]
        block = r.w2.at[h, pl.ds(pl.multiple_of(start, 32), size)]
        peer = (s, lax.rem(h + t, NH))
        return remote(block, block, r.w2_send.at[t, i], r.w2_recv.at[t, i], peer)

    def w2_on(t, i):
        start, size = pieces[i]
        block = r.w2.at[lax.rem(h + NH - t, NH), pl.ds(pl.multiple_of(start, 32), size)]
        return remote(block, block, r.w2_on_send.at[t, i], r.w2_on_recv.at[t, i], twin)

    halves = [(t, i) for t in (2, 1, 3) for i in range(3)]
    for t, i in halves:
        w2_to(t, i).start()

    def pack_q(i, carry):
        d = lax.rem(i + 2, NX)
        column = lax.rem(x + d, NX)
        queries = matmul(column_rows(column), r.packed[:, 512:640])
        queries = queries.astype(BF16).reshape(NY, NC, SLOTS, 128)

        @pl.when(d != 0)
        def _():
            r.out_q[column] = queries

        @pl.when(d == 0)
        def _():
            for n in range(NY):
                for e in range(NC):
                    r.mid_q[n, e, x] = queries[n, e]

        return carry

    lax.fori_loop(0, NX, pack_q, 0)
    others = [(d, e) for d in (2, 1, 3, 0) for e in range(NC) if (d, e) != (0, 0)]
    for first, then in ((k1, k2), (v1, v2)):
        for d in (1, 2, 3):
            first(d).wait_recv()
        for d, e in others:
            then(d, e).start()

    for d in (2, 1, 3):
        q1(d).start()
    r.in_k[y, c] = r.mid_k[y, c]
    for n in range(NY):
        r.in_v[n, c, x] = r.mid_v[x, c, n]
    for then in (k2, v2):
        for d, e in others:
            then(d, e).wait_recv()

    for t, i in halves:
        w2_to(t, i).wait_recv()
        w2_on(t, i).start()

    def settle(g, carry):
        at = (g // NC, lax.rem(g, NC))
        lane = lax.broadcasted_iota(jnp.int32, (NX, SLOTS, 128), 2)
        other = r.in_k[(*at, slice(None), slice(None), slice(128, 256))].astype(F32)
        third = r.in_v[(*at, slice(None), slice(None), slice(128, 256))]
        marks = jnp.where(lane < 68, FAR * (1.0 - other), 0.0)
        r.q_third[at] = jnp.where(lane < 64, third.astype(F32), marks).astype(BF16)
        r.in_v[(*at, slice(None), slice(None), slice(128, 256))] = jnp.where(
            lane < 64, jnp.ones_like(third), third
        )
        return carry

    lax.fori_loop(0, NGROUP, settle, 0)
    for d in (1, 2, 3):
        q1(d).wait_recv()
    for d, e in ((0, 1), (3, 0), (3, 1), (2, 0), (2, 1), (1, 0), (1, 1)):
        q2(d, e).start()
    r.in_q[y, c] = r.mid_q[y, c]

    def group(i):
        return lax.rem(y + i // NC, NY) * NC + lax.rem(c + i, NC)

    def score(i, head):
        g = group(i)
        at = (g // NC, lax.rem(g, NC))
        queries = jnp.concatenate(
            [r.in_q[at].reshape(GROWS, 128), r.q_third[at].reshape(GROWS, 128)], axis=1
        )
        keys = r.in_k[...].reshape(NS * SLOTS, 256)
        r.scores[head] = matmul(only_head(queries, head), keys, NT)

    def weigh(head):
        scores = r.scores[head]
        highest = jnp.max(scores, axis=1, keepdims=True)
        weights = jnp.exp2(scores - highest).astype(BF16)
        sums = matmul(weights, r.in_v[...].reshape(NS * SLOTS, 256))
        return sums * (1.0 / sums[:, 128:129])

    score(0, 0)

    def attend1(i, carry, last=False):
        g = group(i)
        if not last:
            q2(lax.rem(NY - (i + 1) // NC, NY), lax.rem(i + 1, NC)).wait_recv()
        scaled = []
        for head in range(3):
            if not (last and head == 2):
                score(i + (head + 1) // 3, (head + 1) % 3)
            scaled.append(weigh(head))
        firsts = jnp.where(lanes((GROWS, 128)) < 64, scaled[0][:, 0:128], scaled[1][:, 0:128])
        third = scaled[2][:, 128:256]
        for j in range(GROUP):
            k = (g // NC) * (NX * NC) + j * NC + lax.rem(g, NC)
            rows = slice(j * SLOTS, (j + 1) * SLOTS)
            a_part = firsts[rows].astype(BF16)
            b_part = packed_third(third[rows]).astype(BF16)
            r.answer[k, 0:SLOTS, :] = a_part
            r.answer[k, SLOTS:ANSWER, :] = b_part

            @pl.when(k != s)
            def _():
                answer_to(k, s).start()

            @pl.when(k == s)
            def _():
                r.back[k, 0:SLOTS, :] = a_part
                r.back[k, SLOTS:ANSWER, :] = b_part

        return carry

    lax.fori_loop(0, NGROUP - 1, attend1, 0)
    attend1(NGROUP - 1, 0, last=True)

    def arrive_back(g, carry):
        for j in range(4):
            k = 4 * g + j

            @pl.when(k != s)
            def _():
                answer_to(k, k).wait_recv()

        block = r.back[pl.ds(4 * g, 4)]
        rows = pl.ds(pl.multiple_of(g * PAIR, PAIR), PAIR)
        third = block[:, SLOTS:ANSWER, :]
        turned = half_turn(third.astype(F32).reshape(HALF, 128)).astype(BF16)
        turned = turned.reshape(4, SLOTS // 2, 128)
        r.back_all[rows, 0:128] = block[:, 0:SLOTS, :].reshape(PAIR, 128)
        r.back_all[rows, 128:256] = jnp.concatenate([turned, third], axis=1).reshape(PAIR, 128)
        return carry

    lax.fori_loop(0, NS // 4, arrive_back, 0)

    def att1_to(t):
        peer = lax.rem(h + t, NH)
        return remote(r.own1.at[peer], r.att1.at[h], r.att1_send.at[t], r.att1_recv.at[t], (s, peer))

    def att1_from(t):
        source = lax.rem(h + NH - t, NH)
        return remote(
            r.own1.at[source], r.att1.at[source], r.att1_send.at[t], r.att1_recv.at[t], (s, source)
        )

    def unpack(t):
        p = lax.rem(h + t, NH)
        rows = pl.ds(pl.multiple_of(p * PAIR, PAIR), PAIR)
        own = matmul(r.chosen_back[rows, :], r.back_all[...])
        return p, own[:, 0:128].astype(BF16), packed_third(own[:, 128:256]).astype(BF16)

    for t in (2, 1, 3):
        p, first, third = unpack(t)
        r.own1[p, 0:PAIR, :] = first
        r.own1[p, PAIR:PACKED, :] = third
        att1_to(t).start()
    _, first, third = unpack(0)
    r.att1[h, 0:PAIR, :] = first
    r.att1[h, PAIR:PACKED, :] = third
    for t in range(1, NH):
        att1_from(t).wait_recv()
    quarter = pl.ds(pl.multiple_of(h * PAIR, PAIR), PAIR)
    total = matmul(gathered_rows([r.att1[g] for g in range(NH)]), r.wo[1])
    r.x2[...] = (total + r.x1[quarter, :].astype(F32)).astype(BF16)

    halos2 = [
        remote(
            r.x2.at[pl.ds(PAIR - HALF, HALF)],
            r.halo2.at[0],
            r.halo2_send.at[0],
            r.halo2_recv.at[0],
            after,
        ),
        remote(
            r.x2.at[pl.ds(0, HALF)], r.halo2.at[1], r.halo2_send.at[1], r.halo2_recv.at[1], before
        ),
    ]
    for copy in halos2:
        copy.start()
    for t, i in halves:
        w2_on(t, i).wait_recv()
    normed = row_normed(r.x2[...])
    inner = pl.ds(HALF, PAIR)
    for g in range(NH):
        projected = matmul(normed, r.w2[g], NT)
        r.q2[g] = (projected[:, 0:256] * Q_SCALE).astype(BF16)
        keep_keys(projected[:, 256:768], r.k2.at[g, inner], r.v2.at[g, inner])
    def edge2(side):
        halos2[side].wait()
        normed = row_normed(r.halo2[side])
        outer = pl.ds(side * (PAIR + HALF), HALF)
        for g in range(NH):
            projected = matmul(normed, r.w2[g, 256:768, :], NT)
            keep_keys(projected, r.k2.at[g, outer], r.v2.at[g, outer])

    def x3_to(b, t):
        block = r.x3.at[pl.ds(pl.multiple_of(h * PAIR + b * HALF, HALF), HALF)]
        peer = (s, lax.rem(h + t, NH))
        return remote(block, block, r.x3_send.at[b, t], r.x3_recv.at[b, t], peer)

    def x3_on(b, t):
        source = lax.rem(h + NH - t, NH)
        half = HALF // 2
        block = r.x3.at[
            pl.ds(pl.multiple_of(source * PAIR + b * HALF + half * (t // 2), half), half)
        ]
        peer = (s, lax.rem(h + t, NH))
        return remote(block, block, r.x3_send.at[b, t - 1], r.x3_recv.at[b, t - 1], peer)

    def write(b, t):
        rows = pl.ds(pl.multiple_of(lax.rem(h + t, NH) * PAIR + b * HALF, HALF), HALF)
        return pltpu.make_async_copy(r.x3.at[rows], out_hbm.at[rows], r.out_sems.at[b, t])

    for b in range(2):
        edge2(b)
        begin = b * HALF
        firsts, thirds = [], []
        for g in range(NH):
            first, third = window_block(
                r.q2[g, begin : begin + HALF, :],
                r.k2[g, begin : begin + 3 * HALF, :],
                r.v2[g, begin : begin + 3 * HALF, :],
                s * ROWS + h * PAIR + begin - HALF,
            )
            firsts.append(first)
            thirds.append(third)
        low = lanes((HALF, 128)) < 64
        for g in (0, 2):
            firsts.append(jnp.where(low, half_turn(thirds[g]), thirds[g + 1]))
        gathered = jnp.concatenate([first.astype(BF16) for first in firsts], axis=1)
        total = matmul(gathered, r.wo[2]) + r.x2[begin : begin + HALF, :].astype(F32)
        rows = pl.ds(pl.multiple_of(h * PAIR + begin, HALF), HALF)
        r.x3[rows, :] = total.astype(BF16)
        for t in (1, 3):
            x3_to(b, t).start()
        write(b, 0).start()
    for b in range(2):
        for t in (1, 3):
            x3_to(b, t).wait_recv()
        for t in (1, 3):
            x3_on(b, t).start()
        for t in (1, 3):
            write(b, t).start()
    for b in range(2):
        for t in (1, 3):
            x3_on(b, t).wait_recv()
        write(b, 2).start()

    def sent(k, carry):
        @pl.when(k != s)
        def _():
            answer_to(k, s).wait_send()

        return carry

    lax.fori_loop(0, NS, sent, 0)
    for t, i in halves:
        w2_to(t, i).wait_send()
        w2_on(t, i).wait_send()
    for d in (1, 2, 3):
        for first in (k1, v1, q1):
            first(d).wait_send()
    for d, e in others:
        for then in (k2, v2, q2):
            then(d, e).wait_send()
    for p in range(NPAIR):
        for t in (1, 3):
            att0_to(p, t).wait_send()
            att0_on(p, t).wait_send()
    for t in range(1, NH):
        att1_to(t).wait_send()
    for b in range(2):
        for t in (1, 3):
            x3_to(b, t).wait_send()
            x3_on(b, t).wait_send()
        for t in range(NH):
            write(b, t).wait()


def shards(tokens, cluster_of, w_query, w_key, w_value, w_out):
    anywhere = pl.BlockSpec(memory_space=pl.ANY)
    return pl.pallas_call(
        kernel,
        out_shape=jax.ShapeDtypeStruct((ROWS, D), BF16),
        in_specs=[anywhere, pl.BlockSpec(memory_space=pltpu.VMEM)] + [anywhere] * 4,
        out_specs=anywhere,
        scratch_shapes=list(SCRATCH.values()),
        compiler_params=pltpu.CompilerParams(
            collective_id=0, has_side_effects=True, vmem_limit_bytes=VMEM_LIMIT
        ),
        name="three_layers",
    )(tokens, cluster_of.reshape(1, ROWS), w_query, w_key, w_value, w_out)


def solution(mesh):
    placed = (
        P("seq", None),
        P("seq"),
        P(None, "head", None),
        P(None, "head", None),
        P(None, "head", None),
        P(),
    )
    return jax.shard_map(
        shards, mesh=mesh, in_specs=placed, out_specs=P("seq", None), check_vma=False
    )
```
